32 devices in a mesh: node: 8 (over y, x, core), local: 4 (over z).
Axes of the slice: x: 2, y: 2, z: 4, core: 2. Of those that a mesh axis runs over, the one named last changes fastest.
Arguments:
- activations: bfloat16 [4096, 4096], P(('node', 'local')), may hold values from -6 to 6
- codes: bfloat16 [16, 256, 128], P('local'), may hold values from -127 to 127, as said below
- scales: float32 [16, 128], P('local'), may hold values from 5e-05 to 0.0005
- cotangent: bfloat16 [4096, 128], P(('node', 'local')), may hold values from -6 to 6
Outputs:
- values_out: bfloat16 [4096, 128], P(('node', 'local'))
- weight_grad: float32 [4096, 128], P(('node', 'local'))
The draws below stay inside these ranges and needn't reach their ends.
Inputs may be any that keep to these rules, and one draw needn't show every extreme that they name: codes are whole numbers.
All inputs are finite; a program needn't handle non-finite values.
Results may differ from the reference program's by a relative error of at most 0.0048.
Values may be sent and summed in bfloat16 or wider, within the bound.
A program may use at most 64 MiB of HBM per device.

```python
import math
import jax
import jax.numpy as jnp
from jax import lax

D = 4096
HD = 128
BLOCK = 256
TOK_DEV = 128
BLOCKS = 16
TOKENS = 4096
N_NODE = 8
N_LOCAL = 4


def draw_codes(key, part):
    key = jax.random.fold_in(key, 11)
    whole = jax.random.randint(key, (BLOCKS, BLOCK, HD), -127, 128)
    return whole.astype(jnp.float32).astype(jnp.bfloat16)


def raised(values, rng, source, target, shards_of, factor):
    def block_of(axis_at):
        return (jnp.arange(values.shape[axis_at]) // (values.shape[axis_at] // shards_of)).reshape((-1,) + (1,) * (values.ndim - 1 - axis_at))

    near = jax.random.permutation(rng, shards_of)[block_of(target)]
    second = (block_of(target) + shards_of // 2) % shards_of
    return jnp.where((block_of(source) == near) | (block_of(source) == second), factor * values, values)


def shard_levels(rng, shape, split, smallest, top_value):
    gain, own = 1.0, jax.random.fold_in(rng, 6)
    for axis_at, shards_of in split:
        steps = jnp.exp(jax.random.uniform(jax.random.fold_in(own, axis_at), (shards_of,), jnp.float32, smallest / len(split), top_value / len(split)))
        gain = gain * jnp.repeat(steps, shape[axis_at] // shards_of).reshape([-1 if axis == axis_at else 1 for axis in range(len(shape))])
    return gain


def noise(key, shape, width, bound, shards=(), dtype=jnp.bfloat16):
    level = shard_levels(key, shape, shards, -0.22, 0.18) if shards else 1.0
    array = jax.random.normal(key, shape, jnp.float32) * width * level
    return jnp.minimum(jnp.maximum(array, -bound), bound).astype(dtype)


def heavy_noise(key, shape, spread, most, cuts, heavy, kind=jnp.bfloat16):
    values = spread * jax.random.normal(key, shape, jnp.float32)
    if cuts:
        values = values * shard_levels(key, shape, cuts, -0.22, 0.18)
    return jnp.clip(raised(values, jax.random.fold_in(key, 3), *heavy), -most, most).astype(kind)


def setup_inputs(seed: int = 0) -> dict:
    arg_keys = jax.random.split(jax.random.key(seed), 5)
    activations = heavy_noise(arg_keys[0], (TOKENS, D), 1.0, 6.0, ((0, 32),), (0, 1, 32, 2.75))
    codes = draw_codes(jax.random.fold_in(arg_keys[4], 71), 0)
    scales = jnp.clip(jnp.exp(math.log(0.0005) - 2.3025852 * jax.random.uniform(arg_keys[2], (BLOCKS, HD), jnp.float32) ** shard_levels(arg_keys[2], (BLOCKS, HD), ((0, 4),), -0.2, 0.2)), 4.999999873689376e-05, 0.0005)
    cotangent = noise(arg_keys[3], (TOKENS, HD), 1.0, 6.0, ((0, 32),))
    return dict(activations=activations, codes=codes, scales=scales, cotangent=cotangent)


def dequantize(codes, scales):
    weight = codes.astype(jnp.float32) * scales[:, None, :]
    return weight.astype(jnp.bfloat16).reshape(-1, codes.shape[2])


def reference(activations, codes, scales, cotangent):
    weight = dequantize(codes, scales)
    groups = N_NODE * N_LOCAL
    act_blocks = activations.reshape(groups, TOK_DEV, D)
    cot_blocks = cotangent.reshape(groups, TOK_DEV, HD)

    def step(total, pair):
        rows, grads = pair
        values = jnp.dot(rows, weight, preferred_element_type=jnp.float32).astype(jnp.bfloat16)
        term = lax.dot_general(rows, grads, (((0,), (0,)), ((), ())), preferred_element_type=jnp.float32)
        return total + term, values

    start = jnp.zeros((D, HD), jnp.float32)
    total, values = lax.scan(step, start, (act_blocks, cot_blocks))
    weight_grad = total * (float(TOKENS) ** -0.5)
    return values.reshape(TOKENS, HD), weight_grad
```

```python
import functools

import jax
import jax.numpy as jnp
from jax import lax
from jax.experimental import pallas as pl
from jax.experimental.pallas import tpu as pltpu
from jax.sharding import PartitionSpec as P

MESH = pl.DeviceIdType.MESH
F32 = jnp.float32
BF16 = jnp.bfloat16


def aligned(value, unit):
    return pl.multiple_of(value * unit, unit)


def exchange_kernel(
    n_node, n_local, norm,
    act_hbm, codes_ref, scales_ref, cot_ref,
    values_ref, grad_ref,
    act, weight, act_in, cot_in, term_out, term_in,
    load_sem, act_send, act_recv, cot_send, cot_recv,
    w_send, w_recv, f_send, f_recv, g_send, g_recv,
):
    node, z = lax.axis_index("node"), lax.axis_index("local")
    pair, core = node // 2, node % 2
    n_pair = n_node // 2
    tok = act.shape[0]
    share = term_in.shape[1]
    blocks, block, width = codes_ref.shape
    rows = blocks * block
    half = rows // 2

    load = pltpu.make_async_copy(act_hbm, act, load_sem)
    load.start()

    peers = []
    for slot in range(1, n_node):
        to = ((pair + slot // 2) % n_pair) * 2 + (core + slot % 2) % 2
        peers.append((slot, to))
    line = [(k, (z + 1 + k) % n_local, (z + n_local - 1 - k) % n_local) for k in range(n_local - 1)]

    barrier = pltpu.get_barrier_semaphore()
    for _, to in peers:
        pl.semaphore_signal(barrier, inc=1, device_id=(to, z), device_id_type=MESH)
    for _, to, _ in line:
        pl.semaphore_signal(barrier, inc=1, device_id=(node, to), device_id_type=MESH)

    for b in range(blocks):
        part = codes_ref[b].astype(F32) * scales_ref[b : b + 1, :]
        weight[z, b * block : (b + 1) * block, :] = part.astype(BF16)
    cot_in[0:tok, :] = cot_ref[...]
    load.wait()
    pl.semaphore_wait(barrier, len(peers) + len(line))

    def cot_copy(slot, to):
        return pltpu.make_async_remote_copy(
            src_ref=cot_ref, dst_ref=cot_in.at[pl.ds(slot * tok, tok)],
            send_sem=cot_send.at[slot], recv_sem=cot_recv.at[slot],
            device_id=(to, z), device_id_type=MESH)

    def act_copy(k, slot, to):
        column = aligned(to * n_local + (z + 1 + k) % n_local, share)
        return pltpu.make_async_remote_copy(
            src_ref=act.at[:, pl.ds(column, share)],
            dst_ref=act_in.at[k, pl.ds(slot * tok, tok)],
            send_sem=act_send.at[k, slot], recv_sem=act_recv.at[k, slot],
            device_id=(to, z), device_id_type=MESH)

    def weight_copy(k, owner, to):
        ref = weight.at[owner, pl.ds(aligned(core, half), half)]
        return pltpu.make_async_remote_copy(
            src_ref=ref, dst_ref=ref, send_sem=w_send.at[k], recv_sem=w_recv.at[k],
            device_id=(node, to), device_id_type=MESH)

    def pass_copy(k, owner, which):
        ref = weight.at[owner, pl.ds(aligned(which, half), half)]
        return pltpu.make_async_remote_copy(
            src_ref=ref, dst_ref=ref, send_sem=f_send.at[k], recv_sem=f_recv.at[k],
            device_id=(pair * 2 + 1 - core, z), device_id_type=MESH)

    def term_copy(k, to):
        return pltpu.make_async_remote_copy(
            src_ref=term_out.at[k], dst_ref=term_in.at[k],
            send_sem=g_send.at[k], recv_sem=g_recv.at[k],
            device_id=(node, to), device_id_type=MESH)

    for slot, to in peers:
        cot_copy(slot, to).start()
    for k, to, _ in line:
        weight_copy(k, z, to).start()
    for k in range(n_local):
        for slot, to in peers:
            act_copy(k, slot, to).start()

    def projected(owner):
        return jnp.dot(act[:, pl.ds(aligned(owner, rows), rows)], weight[owner],
                       preferred_element_type=F32)

    total = projected(z)

    def group_term(k):
        column = aligned(node * n_local + (z + 1 + k) % n_local, share)
        act_in[k, 0:tok, :] = act[:, pl.ds(column, share)]
        for slot, to in peers:
            if k == 0:
                cot_copy(slot, to).wait_recv()
            act_copy(k, slot, to).wait_recv()
        return lax.dot_general(act_in[k], cot_in[...], (((0,), (0,)), ((), ())),
                               preferred_element_type=F32)

    for k, to, _ in line:
        term_out[k] = group_term(k)
        term_copy(k, to).start()
    for k, to, owner in line:
        weight_copy(k, owner, to).wait_recv()
        pass_copy(k, owner, core).start()
    grad = group_term(n_local - 1)
    for k, to, owner in line:
        pass_copy(k, owner, 1 - core).wait_recv()
        total += projected(owner)
    values_ref[...] = total.astype(BF16)
    for k, to, _ in line:
        term_copy(k, to).wait_recv()
        grad += term_in[k]
    grad_ref[...] = grad * norm

    for slot, to in peers:
        cot_copy(slot, to).wait_send()
        for k in range(n_local):
            act_copy(k, slot, to).wait_send()
    for k, to, owner in line:
        weight_copy(k, z, to).wait_send()
        pass_copy(k, owner, core).wait_send()
        term_copy(k, to).wait_send()


def exchanged(n_node, n_local, activations, codes, scales, cotangent):
    tok, width = activations.shape
    blocks, block, head = codes.shape
    rows = blocks * block
    share = width // (n_node * n_local)
    dma = pltpu.SemaphoreType.DMA
    vmem = pl.BlockSpec(memory_space=pltpu.VMEM)
    norm = float(tok * n_node * n_local) ** (-0.5)
    return pl.pallas_call(
        functools.partial(exchange_kernel, n_node, n_local, norm),
        out_shape=(
            jax.ShapeDtypeStruct((tok, head), BF16),
            jax.ShapeDtypeStruct((share, head), F32),
        ),
        in_specs=[pl.BlockSpec(memory_space=pl.ANY), vmem, vmem, vmem],
        out_specs=(vmem, vmem),
        scratch_shapes=[
            pltpu.VMEM((tok, width), BF16),
            pltpu.VMEM((n_local, rows, head), BF16),
            pltpu.VMEM((n_local, n_node * tok, share), BF16),
            pltpu.VMEM((n_node * tok, head), BF16),
            pltpu.VMEM((n_local, share, head), F32),
            pltpu.VMEM((n_local, share, head), F32),
            dma, dma((n_local, n_node)), dma((n_local, n_node)), dma((n_node,)), dma((n_node,)),
            dma((n_local,)), dma((n_local,)), dma((n_local,)), dma((n_local,)),
            dma((n_local,)), dma((n_local,)),
        ],
        compiler_params=pltpu.CompilerParams(
            collective_id=0, has_side_effects=True, vmem_limit_bytes=32 * 1024 * 1024
        ),
        cost_estimate=pl.CostEstimate(
            flops=4 * tok * width * head, bytes_accessed=2 * tok * width, transcendentals=0
        ),
    )(activations, codes, scales, cotangent)


def gathered(n_node, n_local, activations, codes, scales, cotangent):
    head = codes.shape[2]
    stored = (codes.astype(F32) * scales[:, None, :]).astype(BF16).reshape(-1, head)
    weight = lax.all_gather(stored, "local", axis=0, tiled=True)
    values = jnp.dot(activations, weight, preferred_element_type=F32).astype(BF16)
    term = lax.dot_general(
        activations, cotangent, (((0,), (0,)), ((), ())), preferred_element_type=F32
    )
    tokens = activations.shape[0] * n_node * n_local
    term = term * float(tokens) ** (-0.5)
    share = term.shape[0] // (n_node * n_local)
    term = term.reshape(n_node, n_local, share, head)
    term = lax.psum_scatter(term, "local", scatter_dimension=1, tiled=True)
    term = lax.psum_scatter(term, "node", scatter_dimension=0, tiled=True)
    return values, term.reshape(share, head)


def solution(mesh):
    n_node, n_local = mesh.shape["node"], mesh.shape["local"]

    def on_device(activations, codes, scales, cotangent):
        share = activations.shape[1] // (n_node * n_local)
        run = exchanged if share % 128 == 0 and n_node % 2 == 0 else gathered
        return run(n_node, n_local, activations, codes, scales, cotangent)

    return jax.shard_map(
        on_device,
        mesh=mesh,
        in_specs=(
            P(("node", "local"), None),
            P("local", None, None),
            P("local", None),
            P(("node", "local"), None),
        ),
        out_specs=(P(("node", "local"), None), P(("node", "local"), None)),
        check_vma=False,
    )
```

```python
import functools

import jax
import jax.numpy as jnp
from jax import lax
from jax.experimental import pallas as pl
from jax.experimental.pallas import tpu as pltpu
from jax.sharding import PartitionSpec as P

MESH = pl.DeviceIdType.MESH
F32 = jnp.float32
BF16 = jnp.bfloat16


def aligned(value, unit):
    return pl.multiple_of(value * unit, unit)


def exchange_kernel(
    n_node, n_local, norm,
    act_hbm, codes_hbm, scales_hbm, cot_hbm,
    values_ref, grad_ref,
    act, codes_ref, scales_ref, cot_ref, weight, act_in, cot_in, term_out, term_in,
    load_sem, act_send, act_recv, cot_send, cot_recv,
    w_send, w_recv, f_send, f_recv, g_send, g_recv,
):
    node, z = lax.axis_index("node"), lax.axis_index("local")
    pair, core = node // 2, node % 2
    n_pair = n_node // 2
    tok = act.shape[0]
    share = term_in.shape[1]
    blocks, block, width = codes_ref.shape
    rows = blocks * block
    half = rows // 2

    loads = [
        pltpu.make_async_copy(there, here, load_sem.at[i])
        for i, (there, here) in enumerate((
            (codes_hbm, codes_ref), (scales_hbm, scales_ref), (cot_hbm, cot_ref), (act_hbm, act)))
    ]
    for load in loads:
        load.start()

    peers = []
    for slot in range(1, n_node):
        to = ((pair + slot // 2) % n_pair) * 2 + (core + slot % 2) % 2
        peers.append((slot, to))
    line = [(k, (z + 1 + k) % n_local, (z + n_local - 1 - k) % n_local) for k in range(n_local - 1)]

    barrier = pltpu.get_barrier_semaphore()
    for _, to in peers:
        pl.semaphore_signal(barrier, inc=1, device_id=(to, z), device_id_type=MESH)
    for _, to, _ in line:
        pl.semaphore_signal(barrier, inc=1, device_id=(node, to), device_id_type=MESH)

    loads[0].wait()
    loads[1].wait()
    for b in range(blocks):
        part = codes_ref[b].astype(F32) * scales_ref[b : b + 1, :]
        weight[z, b * block : (b + 1) * block, :] = part.astype(BF16)
    loads[2].wait()
    cot_in[0:tok, :] = cot_ref[...]
    loads[3].wait()
    pl.semaphore_wait(barrier, len(peers) + len(line))

    def cot_copy(slot, to):
        return pltpu.make_async_remote_copy(
            src_ref=cot_ref, dst_ref=cot_in.at[pl.ds(slot * tok, tok)],
            send_sem=cot_send.at[slot], recv_sem=cot_recv.at[slot],
            device_id=(to, z), device_id_type=MESH)

    def act_copy(k, slot, to):
        column = aligned(to * n_local + (z + 1 + k) % n_local, share)
        return pltpu.make_async_remote_copy(
            src_ref=act.at[:, pl.ds(column, share)],
            dst_ref=act_in.at[k, pl.ds(slot * tok, tok)],
            send_sem=act_send.at[k, slot], recv_sem=act_recv.at[k, slot],
            device_id=(to, z), device_id_type=MESH)

    def weight_copy(k, owner, to):
        ref = weight.at[owner, pl.ds(aligned(core, half), half)]
        return pltpu.make_async_remote_copy(
            src_ref=ref, dst_ref=ref, send_sem=w_send.at[k], recv_sem=w_recv.at[k],
            device_id=(node, to), device_id_type=MESH)

    def pass_copy(k, owner, which):
        ref = weight.at[owner, pl.ds(aligned(which, half), half)]
        return pltpu.make_async_remote_copy(
            src_ref=ref, dst_ref=ref, send_sem=f_send.at[k], recv_sem=f_recv.at[k],
            device_id=(pair * 2 + 1 - core, z), device_id_type=MESH)

    def term_copy(k, to):
        return pltpu.make_async_remote_copy(
            src_ref=term_out.at[k], dst_ref=term_in.at[k],
            send_sem=g_send.at[k], recv_sem=g_recv.at[k],
            device_id=(node, to), device_id_type=MESH)

    for slot, to in peers:
        cot_copy(slot, to).start()
    for k, to, _ in line:
        weight_copy(k, z, to).start()
    for k in range(n_local):
        for slot, to in peers:
            act_copy(k, slot, to).start()

    def projected(owner):
        return jnp.dot(act[:, pl.ds(aligned(owner, rows), rows)], weight[owner],
                       preferred_element_type=F32)

    total = projected(z)

    def group_term(k):
        column = aligned(node * n_local + (z + 1 + k) % n_local, share)
        act_in[k, 0:tok, :] = act[:, pl.ds(column, share)]
        for slot, to in peers:
            if k == 0:
                cot_copy(slot, to).wait_recv()
            act_copy(k, slot, to).wait_recv()
        return lax.dot_general(act_in[k], cot_in[...], (((0,), (0,)), ((), ())),
                               preferred_element_type=F32)

    for k, to, _ in line:
        term_out[k] = group_term(k)
        term_copy(k, to).start()
    for k, to, owner in line:
        weight_copy(k, owner, to).wait_recv()
        pass_copy(k, owner, core).start()
    grad = group_term(n_local - 1)
    for k, to, owner in line:
        pass_copy(k, owner, 1 - core).wait_recv()
        total += projected(owner)
    values_ref[...] = total.astype(BF16)
    for k, to, _ in line:
        term_copy(k, to).wait_recv()
        grad += term_in[k]
    grad_ref[...] = grad * norm

    for slot, to in peers:
        cot_copy(slot, to).wait_send()
        for k in range(n_local):
            act_copy(k, slot, to).wait_send()
    for k, to, owner in line:
        weight_copy(k, z, to).wait_send()
        pass_copy(k, owner, core).wait_send()
        term_copy(k, to).wait_send()


def exchanged(n_node, n_local, activations, codes, scales, cotangent):
    tok, width = activations.shape
    blocks, block, head = codes.shape
    rows = blocks * block
    share = width // (n_node * n_local)
    dma = pltpu.SemaphoreType.DMA
    vmem = pl.BlockSpec(memory_space=pltpu.VMEM)
    norm = float(tok * n_node * n_local) ** (-0.5)
    return pl.pallas_call(
        functools.partial(exchange_kernel, n_node, n_local, norm),
        out_shape=(
            jax.ShapeDtypeStruct((tok, head), BF16),
            jax.ShapeDtypeStruct((share, head), F32),
        ),
        in_specs=[pl.BlockSpec(memory_space=pltpu.HBM)] * 4,
        out_specs=(vmem, vmem),
        scratch_shapes=[
            pltpu.VMEM((tok, width), BF16),
            pltpu.VMEM(codes.shape, BF16),
            pltpu.VMEM(scales.shape, F32),
            pltpu.VMEM(cotangent.shape, BF16),
            pltpu.VMEM((n_local, rows, head), BF16),
            pltpu.VMEM((n_local, n_node * tok, share), BF16),
            pltpu.VMEM((n_node * tok, head), BF16),
            pltpu.VMEM((n_local, share, head), F32),
            pltpu.VMEM((n_local, share, head), F32),
            dma((4,)), dma((n_local, n_node)), dma((n_local, n_node)), dma((n_node,)), dma((n_node,)),
            dma((n_local,)), dma((n_local,)), dma((n_local,)), dma((n_local,)),
            dma((n_local,)), dma((n_local,)),
        ],
        compiler_params=pltpu.CompilerParams(
            collective_id=0, has_side_effects=True, vmem_limit_bytes=32 * 1024 * 1024
        ),
        cost_estimate=pl.CostEstimate(
            flops=4 * tok * width * head, bytes_accessed=2 * tok * width, transcendentals=0
        ),
    )(activations, codes, scales, cotangent)


def gathered(n_node, n_local, activations, codes, scales, cotangent):
    head = codes.shape[2]
    stored = (codes.astype(F32) * scales[:, None, :]).astype(BF16).reshape(-1, head)
    weight = lax.all_gather(stored, "local", axis=0, tiled=True)
    values = jnp.dot(activations, weight, preferred_element_type=F32).astype(BF16)
    term = lax.dot_general(
        activations, cotangent, (((0,), (0,)), ((), ())), preferred_element_type=F32
    )
    tokens = activations.shape[0] * n_node * n_local
    term = term * float(tokens) ** (-0.5)
    share = term.shape[0] // (n_node * n_local)
    term = term.reshape(n_node, n_local, share, head)
    term = lax.psum_scatter(term, "local", scatter_dimension=1, tiled=True)
    term = lax.psum_scatter(term, "node", scatter_dimension=0, tiled=True)
    return values, term.reshape(share, head)


def solution(mesh):
    n_node, n_local = mesh.shape["node"], mesh.shape["local"]

    def on_device(activations, codes, scales, cotangent):
        share = activations.shape[1] // (n_node * n_local)
        run = exchanged if share % 128 == 0 and n_node % 2 == 0 else gathered
        return run(n_node, n_local, activations, codes, scales, cotangent)

    return jax.shard_map(
        on_device,
        mesh=mesh,
        in_specs=(
            P(("node", "local"), None),
            P("local", None, None),
            P("local", None),
            P(("node", "local"), None),
        ),
        out_specs=(P(("node", "local"), None), P(("node", "local"), None)),
        check_vma=False,
    )
```

```python
import functools

import jax
import jax.numpy as jnp
from jax import lax
from jax.experimental import pallas as pl
from jax.experimental.pallas import tpu as pltpu
from jax.sharding import PartitionSpec as P

MESH = pl.DeviceIdType.MESH
F32 = jnp.float32
BF16 = jnp.bfloat16


def aligned(value, unit):
    return pl.multiple_of(value * unit, unit)


def exchange_kernel(
    n_local, norm,
    act_hbm, codes_hbm, scales_hbm, cot_hbm,
    values_ref, grad_ref,
    act, codes_ref, scales_ref, cot_ref, weight, weight_in, act_in, cot_in,
    other_out, other_in, term_out, term_in,
    load_sem, act_send, act_recv, cot_send, cot_recv,
    w_send, w_recv, s_send, s_recv, g_send, g_recv,
):
    node, z = lax.axis_index("node"), lax.axis_index("local")
    y, x, core = node // 4, (node // 2) % 2, node % 2
    tok = act.shape[0]
    share = term_in.shape[1]
    blocks, block, _ = codes_ref.shape
    rows = blocks * block
    quarter = rows // 4
    eighth = quarter // 2
    last = n_local - 1

    loads = [
        pltpu.make_async_copy(there, here, load_sem.at[i])
        for i, (there, here) in enumerate((
            (codes_hbm, codes_ref), (scales_hbm, scales_ref), (cot_hbm, cot_ref), (act_hbm, act)))
    ]
    for load in loads:
        load.start()

    def at(to_y, to_x, to_core):
        return (to_y * 2 + to_x) * 2 + to_core

    partner = at(y, x, 1 - core)
    along_x = (at(y, 1 - x, core), at(y, 1 - x, 1 - core))
    along_y = (at(1 - y, x, core), at(1 - y, x, 1 - core))
    near = (partner,) + along_x + along_y
    line = [(k, (z + 1 + k) % n_local, (z + last - k) % n_local) for k in range(last)]

    barrier = pltpu.get_barrier_semaphore()
    for to in near:
        pl.semaphore_signal(barrier, inc=1, device_id=(to, z), device_id_type=MESH)
    for _, to, _ in line:
        pl.semaphore_signal(barrier, inc=1, device_id=(node, to), device_id_type=MESH)

    loads[0].wait()
    loads[1].wait()
    for b in range(blocks):
        part = codes_ref[b].astype(F32) * scales_ref[b : b + 1, :]
        weight[b * block : (b + 1) * block, :] = part.astype(BF16)
    loads[2].wait()
    cot_in[2 * tok : 3 * tok, :] = cot_ref[...]
    loads[3].wait()
    pl.semaphore_wait(barrier, len(near) + len(line))

    def send(src, dst, send_sem, recv_sem, to_node, to_local):
        return pltpu.make_async_remote_copy(
            src_ref=src, dst_ref=dst, send_sem=send_sem, recv_sem=recv_sem,
            device_id=(to_node, to_local), device_id_type=MESH)

    cot_copies = [
        send(cot_ref, cot_in.at[slot * tok : (slot + 1) * tok], cot_send.at[i], cot_recv.at[i], to, z)
        for i, (to, slot) in enumerate(zip(near, (3, 0, 1, 4, 5)))
    ]

    def column_of(k, owner):
        return pl.ds(aligned(owner * n_local + (z + 1 + k) % n_local, share), share)

    def second_of(k, owner_y, owner_x, owner_core):
        if k % 2 == 0:
            return at(1 - owner_y, owner_x, owner_core)
        return at(owner_y, 1 - owner_x, owner_core)

    def act_copies(k):
        over_x = k % 2 == 0
        first = (y, 1 - x) if over_x else (1 - y, x)
        own_row, first_row = (2, 0) if over_x else (0, 2)
        copies = []
        for i, (to_y, to_x, to_core, row) in enumerate((
            (first[0], first[1], core, first_row),
            (first[0], first[1], 1 - core, first_row + 1),
            (y, x, 1 - core, own_row + 1),
        )):
            to = at(to_y, to_x, to_core)
            for which, owner in ((1, second_of(k, to_y, to_x, to_core)), (0, to)):
                copies.append(send(
                    act.at[:, column_of(k, owner)],
                    act_in.at[k, which, row * tok : (row + 1) * tok],
                    act_send.at[k, 2 * i + which], act_recv.at[k, 2 * i + which], to, z))
        return copies

    def sum_copy(k):
        return send(other_out.at[k], other_in.at[k], s_send.at[k], s_recv.at[k],
                    second_of(k, y, x, core), z)

    def term_copy(k, to):
        return send(term_out.at[k], term_in.at[k], g_send.at[k], g_recv.at[k], node, to)

    parity = (x + y) % 2

    def part_of(of_parity, of_core, begin, size):
        return pl.ds(aligned((of_parity * 2 + of_core) * 2 + begin, eighth), size * eighth)

    def line_copy(k, to):
        part = part_of(parity, core, 0, 2)
        return send(weight.at[part], weight_in.at[k, part], w_send.at[0, k], w_recv.at[0, k], node, to)

    def plane_copies(k, of_parity):
        return [
            send(weight_in.at[k, part], weight_in.at[k, part],
                 w_send.at[1 + i, k], w_recv.at[1 + i, k], to, z)
            for i, (to, part) in enumerate((
                (along_x[0], part_of(of_parity, core, 0, 1)),
                (along_y[0], part_of(of_parity, core, 1, 1))))
        ]

    def pass_copy(k, i, of_parity, of_core):
        part = part_of(of_parity, of_core, 0, 2)
        return send(weight_in.at[k, part], weight_in.at[k, part],
                    w_send.at[3 + i, k], w_recv.at[3 + i, k], partner, z)

    for copy in cot_copies:
        copy.start()
    for k in range(min(2, n_local)):
        for copy in act_copies(k):
            copy.start()
    for k, to, _ in line:
        line_copy(k, to).start()

    def projected(owner, stored):
        return jnp.dot(act[:, pl.ds(aligned(owner, rows), rows)], stored, preferred_element_type=F32)

    total = projected(z, weight[...])

    def group_term(k):
        over_x = k % 2 == 0
        own_row = 2 if over_x else 0
        own = slice(own_row * tok, (own_row + 1) * tok)
        act_in[k, 1, own, :] = act[:, column_of(k, second_of(k, y, x, core))]
        act_in[k, 0, own, :] = act[:, column_of(k, node)]
        if k == 0:
            for copy in cot_copies:
                copy.wait_recv()
        for copy in act_copies(k):
            copy.wait_recv()
        if k + 2 < n_local:
            for copy in act_copies(k + 2):
                copy.start()
        cot = cot_in[0 : 4 * tok, :] if over_x else cot_in[2 * tok : 6 * tok, :]

        def product(which):
            return lax.dot_general(act_in[k, which], cot, (((0,), (0,)), ((), ())),
                                   preferred_element_type=F32)

        other_out[k] = product(1)
        sum_copy(k).start()
        term_out[k] = product(0)

    def finish_term(k):
        sum_copy(k).wait_recv()
        term_out[k] += other_in[k]
        if k < last:
            term_copy(k, line[k][1]).start()

    early = min(2, n_local)
    for k in range(early):
        group_term(k)
    for k, to, _ in line:
        line_copy(k, to).wait_recv()
        for copy in plane_copies(k, parity):
            copy.start()
        pass_copy(k, 0, parity, core).start()
    for k in range(early):
        finish_term(k)
    for k in range(early, n_local):
        group_term(k)
    for k, _, _ in line:
        for copy in plane_copies(k, 1 - parity):
            copy.wait_recv()
        pass_copy(k, 1, 1 - parity, core).start()
    for k in range(early, n_local):
        finish_term(k)
    for k, _, owner in line:
        pass_copy(k, 0, parity, 1 - core).wait_recv()
        pass_copy(k, 1, 1 - parity, 1 - core).wait_recv()
        total += projected(owner, weight_in[k])
    values_ref[...] = total.astype(BF16)
    grad = term_out[last]
    for k, to, _ in line:
        term_copy(k, to).wait_recv()
        grad += term_in[k]
    grad_ref[...] = grad * norm

    for copy in cot_copies:
        copy.wait_send()
    for k in range(n_local):
        for copy in act_copies(k):
            copy.wait_send()
        sum_copy(k).wait_send()
    for k, to, _ in line:
        line_copy(k, to).wait_send()
        for copy in plane_copies(k, parity):
            copy.wait_send()
        pass_copy(k, 0, parity, core).wait_send()
        pass_copy(k, 1, 1 - parity, core).wait_send()
        term_copy(k, to).wait_send()


def exchanged(n_node, n_local, activations, codes, scales, cotangent):
    tok, width = activations.shape
    blocks, block, head = codes.shape
    rows = blocks * block
    share = width // (n_node * n_local)
    dma = pltpu.SemaphoreType.DMA
    vmem = pl.BlockSpec(memory_space=pltpu.VMEM)
    norm = float(tok * n_node * n_local) ** (-0.5)
    piece = pltpu.VMEM((n_local, share, head), F32)
    return pl.pallas_call(
        functools.partial(exchange_kernel, n_local, norm),
        out_shape=(
            jax.ShapeDtypeStruct((tok, head), BF16),
            jax.ShapeDtypeStruct((share, head), F32),
        ),
        in_specs=[pl.BlockSpec(memory_space=pltpu.HBM)] * 4,
        out_specs=(vmem, vmem),
        scratch_shapes=[
            pltpu.VMEM((tok, width), BF16),
            pltpu.VMEM(codes.shape, BF16),
            pltpu.VMEM(scales.shape, F32),
            pltpu.VMEM(cotangent.shape, BF16),
            pltpu.VMEM((rows, head), BF16),
            pltpu.VMEM((n_local - 1, rows, head), BF16),
            pltpu.VMEM((n_local, 2, 4 * tok, share), BF16),
            pltpu.VMEM((6 * tok, head), BF16),
            piece, piece, piece, piece,
            dma((4,)), dma((n_local, 6)), dma((n_local, 6)), dma((5,)), dma((5,)),
            dma((5, n_local)), dma((5, n_local)), dma((n_local,)), dma((n_local,)),
            dma((n_local,)), dma((n_local,)),
        ],
        compiler_params=pltpu.CompilerParams(collective_id=0, has_side_effects=True),
        cost_estimate=pl.CostEstimate(
            flops=4 * tok * width * head, bytes_accessed=2 * tok * width, transcendentals=0
        ),
    )(activations, codes, scales, cotangent)


def gathered(n_node, n_local, activations, codes, scales, cotangent):
    head = codes.shape[2]
    stored = (codes.astype(F32) * scales[:, None, :]).astype(BF16).reshape(-1, head)
    weight = lax.all_gather(stored, "local", axis=0, tiled=True)
    values = jnp.dot(activations, weight, preferred_element_type=F32).astype(BF16)
    term = lax.dot_general(
        activations, cotangent, (((0,), (0,)), ((), ())), preferred_element_type=F32
    )
    tokens = activations.shape[0] * n_node * n_local
    term = term * float(tokens) ** (-0.5)
    share = term.shape[0] // (n_node * n_local)
    term = term.reshape(n_node, n_local, share, head)
    term = lax.psum_scatter(term, "local", scatter_dimension=1, tiled=True)
    term = lax.psum_scatter(term, "node", scatter_dimension=0, tiled=True)
    return values, term.reshape(share, head)


def solution(mesh):
    n_node, n_local = mesh.shape["node"], mesh.shape["local"]

    def on_device(activations, codes, scales, cotangent):
        share = activations.shape[1] // (n_node * n_local)
        rows = codes.shape[0] * codes.shape[1]
        fits = n_node == 8 and n_local > 1 and share % 128 == 0 and rows % 128 == 0
        run = exchanged if fits else gathered
        return run(n_node, n_local, activations, codes, scales, cotangent)

    return jax.shard_map(
        on_device,
        mesh=mesh,
        in_specs=(
            P(("node", "local"), None),
            P("local", None, None),
            P("local", None),
            P(("node", "local"), None),
        ),
        out_specs=(P(("node", "local"), None), P(("node", "local"), None)),
        check_vma=False,
    )
```

```python
import functools

import jax
import jax.numpy as jnp
from jax import lax
from jax.experimental import pallas as pl
from jax.experimental.pallas import tpu as pltpu
from jax.sharding import PartitionSpec as P

MESH = pl.DeviceIdType.MESH
F32 = jnp.float32
BF16 = jnp.bfloat16


def aligned(value, unit):
    return pl.multiple_of(value * unit, unit)


def exchange_kernel(
    n_local, norm,
    act_hbm, codes_hbm, scales_hbm, cot_hbm,
    values_ref, grad_ref,
    act, codes_ref, scales_ref, weight, weight_in, act_in, cot_in,
    other_out, other_in, term_out, term_in,
    load_sem, act_send, act_recv, cot_send, cot_recv,
    w_send, w_recv, s_send, s_recv, g_send, g_recv,
):
    node, z = lax.axis_index("node"), lax.axis_index("local")
    y, x, core = node // 4, (node // 2) % 2, node % 2
    tok = act.shape[0]
    share = term_in.shape[1]
    blocks, block, _ = codes_ref.shape
    rows = blocks * block
    quarter = rows // 4
    eighth = quarter // 2
    last = n_local - 1

    loads = [
        pltpu.make_async_copy(there, here, load_sem.at[i])
        for i, (there, here) in enumerate((
            (codes_hbm, codes_ref), (scales_hbm, scales_ref),
            (cot_hbm, cot_in.at[2 * tok : 3 * tok]), (act_hbm, act)))
    ]
    for load in loads:
        load.start()

    def at(to_y, to_x, to_core):
        return (to_y * 2 + to_x) * 2 + to_core

    partner = at(y, x, 1 - core)
    along_x = (at(y, 1 - x, core), at(y, 1 - x, 1 - core))
    along_y = (at(1 - y, x, core), at(1 - y, x, 1 - core))
    near = (partner,) + along_x + along_y
    line = [(k, (z + 1 + k) % n_local, (z + last - k) % n_local) for k in range(last)]

    barrier = pltpu.get_barrier_semaphore()
    for to in near:
        pl.semaphore_signal(barrier, inc=1, device_id=(to, z), device_id_type=MESH)
    for _, to, _ in line:
        pl.semaphore_signal(barrier, inc=1, device_id=(node, to), device_id_type=MESH)

    pl.semaphore_wait(barrier, len(near) + len(line))

    def send(src, dst, send_sem, recv_sem, to_node, to_local):
        return pltpu.make_async_remote_copy(
            src_ref=src, dst_ref=dst, send_sem=send_sem, recv_sem=recv_sem,
            device_id=(to_node, to_local), device_id_type=MESH)

    def cot_copy(i, source, slot, to):
        return send(source, cot_in.at[slot * tok : (slot + 1) * tok],
                    cot_send.at[i], cot_recv.at[i], to, z)

    cot_copies = [
        cot_copy(i, cot_hbm, slot, to)
        for i, (to, slot) in enumerate(((along_x[0], 0), (along_y[0], 4), (partner, 3)))
    ]
    cot_passes = [
        cot_copy(3 + i, cot_in.at[slot * tok : (slot + 1) * tok], slot + 1, partner)
        for i, slot in enumerate((0, 4))
    ]

    def column_of(k, owner):
        return pl.ds(aligned(owner * n_local + (z + 1 + k) % n_local, share), share)

    def second_of(k, owner_y, owner_x, owner_core):
        if k % 2 == 0:
            return at(1 - owner_y, owner_x, owner_core)
        return at(owner_y, 1 - owner_x, owner_core)

    def act_copies(k):
        over_x = k % 2 == 0
        first = (y, 1 - x) if over_x else (1 - y, x)
        own_row, first_row = (2, 0) if over_x else (0, 2)
        copies = []
        for i, (to_y, to_x, to_core, row) in enumerate((
            (first[0], first[1], core, first_row),
            (first[0], first[1], 1 - core, first_row + 1),
            (y, x, 1 - core, own_row + 1),
        )):
            to = at(to_y, to_x, to_core)
            for which, owner in ((1, second_of(k, to_y, to_x, to_core)), (0, to)):
                copies.append(send(
                    (act_hbm if k < 2 else act).at[:, column_of(k, owner)],
                    act_in.at[k, which, row * tok : (row + 1) * tok],
                    act_send.at[k, 2 * i + which], act_recv.at[k, 2 * i + which], to, z))
        return copies

    def sum_copy(k):
        return send(other_out.at[k], other_in.at[k], s_send.at[k], s_recv.at[k],
                    second_of(k, y, x, core), z)

    def term_copy(k, to):
        return send(term_out.at[k], term_in.at[k], g_send.at[k], g_recv.at[k], node, to)

    parity = (x + y) % 2

    def part_of(of_parity, of_core, begin, size):
        return pl.ds(aligned((of_parity * 2 + of_core) * 2 + begin, eighth), size * eighth)

    def line_copy(k, to):
        part = part_of(parity, core, 0, 2)
        return send(weight.at[part], weight_in.at[k, part], w_send.at[0, k], w_recv.at[0, k], node, to)

    def plane_copies(k, of_parity):
        return [
            send(weight_in.at[k, part], weight_in.at[k, part],
                 w_send.at[1 + i, k], w_recv.at[1 + i, k], to, z)
            for i, (to, part) in enumerate((
                (along_x[0], part_of(of_parity, core, 0, 1)),
                (along_y[0], part_of(of_parity, core, 1, 1))))
        ]

    def pass_copy(k, i, of_parity, of_core):
        part = part_of(of_parity, of_core, 0, 2)
        return send(weight_in.at[k, part], weight_in.at[k, part],
                    w_send.at[3 + i, k], w_recv.at[3 + i, k], partner, z)

    for copy in cot_copies:
        copy.start()
    for k in range(min(2, n_local)):
        for copy in act_copies(k):
            copy.start()

    loads[0].wait()
    loads[1].wait()
    for b in range(blocks):
        part = codes_ref[b].astype(F32) * scales_ref[b : b + 1, :]
        weight[b * block : (b + 1) * block, :] = part.astype(BF16)
    for k, to, _ in line:
        line_copy(k, to).start()
    for load in loads[2:]:
        load.wait()

    def projected(owner, stored):
        return jnp.dot(act[:, pl.ds(aligned(owner, rows), rows)], stored, preferred_element_type=F32)

    total = projected(z, weight[...])

    def group_term(k):
        over_x = k % 2 == 0
        own_row = 2 if over_x else 0
        own = slice(own_row * tok, (own_row + 1) * tok)
        act_in[k, 1, own, :] = act[:, column_of(k, second_of(k, y, x, core))]
        act_in[k, 0, own, :] = act[:, column_of(k, node)]
        if k == 0:
            for i, copy in enumerate(cot_copies):
                copy.wait_recv()
                if i < 2:
                    cot_passes[i].start()
            if n_local > 2:
                for copy in act_copies(2):
                    copy.start()
        for copy in act_copies(k):
            copy.wait_recv()
        if k == 0:
            for copy in cot_passes:
                copy.wait_recv()
        cot = cot_in[0 : 4 * tok, :] if over_x else cot_in[2 * tok : 6 * tok, :]

        def product(which):
            return lax.dot_general(act_in[k, which], cot, (((0,), (0,)), ((), ())),
                                   preferred_element_type=F32)

        other_out[k] = product(1)
        sum_copy(k).start()
        if k + 3 < n_local:
            for copy in act_copies(k + 3):
                copy.start()
        term_out[k] = product(0)

    def finish_term(k):
        sum_copy(k).wait_recv()
        term_out[k] += other_in[k]
        if k < last:
            term_copy(k, line[k][1]).start()

    early = min(2, n_local)
    for k in range(early):
        group_term(k)
    for k, to, _ in line:
        line_copy(k, to).wait_recv()
        for copy in plane_copies(k, parity):
            copy.start()
        pass_copy(k, 0, parity, core).start()
    for k in range(early):
        finish_term(k)
    for k in range(early, n_local):
        group_term(k)
    for k, _, _ in line:
        for copy in plane_copies(k, 1 - parity):
            copy.wait_recv()
        pass_copy(k, 1, 1 - parity, core).start()
    for k in range(early, n_local):
        finish_term(k)
    for k, _, owner in line:
        pass_copy(k, 0, parity, 1 - core).wait_recv()
        pass_copy(k, 1, 1 - parity, 1 - core).wait_recv()
        total += projected(owner, weight_in[k])
    values_ref[...] = total.astype(BF16)
    grad = term_out[last]
    for k, to, _ in line:
        term_copy(k, to).wait_recv()
        grad += term_in[k]
    grad_ref[...] = grad * norm

    for copy in cot_copies + cot_passes:
        copy.wait_send()
    for k in range(n_local):
        for copy in act_copies(k):
            copy.wait_send()
        sum_copy(k).wait_send()
    for k, to, _ in line:
        line_copy(k, to).wait_send()
        for copy in plane_copies(k, parity):
            copy.wait_send()
        pass_copy(k, 0, parity, core).wait_send()
        pass_copy(k, 1, 1 - parity, core).wait_send()
        term_copy(k, to).wait_send()


def hand_over_kernel(values, grad, values_out, grad_out, sem):
    copies = [
        pltpu.make_async_copy(there, here, sem.at[i])
        for i, (there, here) in enumerate(((values, values_out), (grad, grad_out)))
    ]
    for copy in copies:
        copy.start()
    for copy in copies:
        copy.wait()


def exchanged(n_node, n_local, activations, codes, scales, cotangent):
    tok, width = activations.shape
    blocks, block, head = codes.shape
    rows = blocks * block
    share = width // (n_node * n_local)
    dma = pltpu.SemaphoreType.DMA
    vmem = pl.BlockSpec(memory_space=pltpu.VMEM)
    norm = float(tok * n_node * n_local) ** (-0.5)
    piece = pltpu.VMEM((n_local, share, head), F32)
    results = pl.pallas_call(
        functools.partial(exchange_kernel, n_local, norm),
        out_shape=(
            jax.ShapeDtypeStruct((tok, head), BF16),
            jax.ShapeDtypeStruct((share, head), F32),
        ),
        in_specs=[pl.BlockSpec(memory_space=pltpu.HBM)] * 4,
        out_specs=(vmem, vmem),
        scratch_shapes=[
            pltpu.VMEM((tok, width), BF16),
            pltpu.VMEM(codes.shape, BF16),
            pltpu.VMEM(scales.shape, F32),
            pltpu.VMEM((rows, head), BF16),
            pltpu.VMEM((n_local - 1, rows, head), BF16),
            pltpu.VMEM((n_local, 2, 4 * tok, share), BF16),
            pltpu.VMEM((6 * tok, head), BF16),
            piece, piece, piece, piece,
            dma((4,)), dma((n_local, 6)), dma((n_local, 6)), dma((5,)), dma((5,)),
            dma((5, n_local)), dma((5, n_local)), dma((n_local,)), dma((n_local,)),
            dma((n_local,)), dma((n_local,)),
        ],
        compiler_params=pltpu.CompilerParams(collective_id=0, has_side_effects=True),
        cost_estimate=pl.CostEstimate(
            flops=4 * tok * width * head, bytes_accessed=2 * tok * width, transcendentals=0
        ),
    )(activations, codes, scales, cotangent)
    hbm = pl.BlockSpec(memory_space=pltpu.HBM)
    return pl.pallas_call(
        hand_over_kernel,
        out_shape=tuple(jax.ShapeDtypeStruct(r.shape, r.dtype) for r in results),
        in_specs=[hbm] * 2,
        out_specs=(hbm, hbm),
        scratch_shapes=[dma((2,))],
    )(*results)


def gathered(n_node, n_local, activations, codes, scales, cotangent):
    head = codes.shape[2]
    stored = (codes.astype(F32) * scales[:, None, :]).astype(BF16).reshape(-1, head)
    weight = lax.all_gather(stored, "local", axis=0, tiled=True)
    values = jnp.dot(activations, weight, preferred_element_type=F32).astype(BF16)
    term = lax.dot_general(
        activations, cotangent, (((0,), (0,)), ((), ())), preferred_element_type=F32
    )
    tokens = activations.shape[0] * n_node * n_local
    term = term * float(tokens) ** (-0.5)
    share = term.shape[0] // (n_node * n_local)
    term = term.reshape(n_node, n_local, share, head)
    term = lax.psum_scatter(term, "local", scatter_dimension=1, tiled=True)
    term = lax.psum_scatter(term, "node", scatter_dimension=0, tiled=True)
    return values, term.reshape(share, head)


def solution(mesh):
    n_node, n_local = mesh.shape["node"], mesh.shape["local"]

    def on_device(activations, codes, scales, cotangent):
        share = activations.shape[1] // (n_node * n_local)
        rows = codes.shape[0] * codes.shape[1]
        fits = n_node == 8 and n_local > 1 and share % 128 == 0 and rows % 128 == 0
        run = exchanged if fits else gathered
        return run(n_node, n_local, activations, codes, scales, cotangent)

    return jax.shard_map(
        on_device,
        mesh=mesh,
        in_specs=(
            P(("node", "local"), None),
            P("local", None, None),
            P("local", None),
            P(("node", "local"), None),
        ),
        out_specs=(P(("node", "local"), None), P(("node", "local"), None)),
        check_vma=False,
    )
```

```python
import functools

import jax
import jax.numpy as jnp
from jax import lax
from jax.experimental import pallas as pl
from jax.experimental.pallas import tpu as pltpu
from jax.sharding import PartitionSpec as P

MESH = pl.DeviceIdType.MESH
F32 = jnp.float32
BF16 = jnp.bfloat16


def aligned(value, unit):
    return pl.multiple_of(value * unit, unit)


def exchange_kernel(
    n_local, norm,
    act_hbm, codes_hbm, scales_hbm, cot_hbm,
    values_ref, grad_ref,
    act, codes_ref, scales_ref, cot_ref, weight, weight_in, act_in, cot_t, cot_in,
    other_out, other_in, term_out, term_in, total,
    load_sem, act_send, act_recv, cot_send, cot_recv,
    w_send, w_recv, s_send, s_recv, g_send, g_recv,
):
    node, z = lax.axis_index("node"), lax.axis_index("local")
    y, x, core = node // 4, (node // 2) % 2, node % 2
    tok = act.shape[0]
    share = grad_ref.shape[0]
    blocks, block, _ = codes_ref.shape
    rows = blocks * block
    quarter = rows // 4
    eighth = quarter // 2
    last = n_local - 1

    loads = [
        pltpu.make_async_copy(there, here, load_sem.at[i])
        for i, (there, here) in enumerate((
            (codes_hbm, codes_ref), (scales_hbm, scales_ref),
            (cot_hbm, cot_ref), (act_hbm, act)))
    ]
    for load in loads:
        load.start()

    def at(to_y, to_x, to_core):
        return (to_y * 2 + to_x) * 2 + to_core

    partner = at(y, x, 1 - core)
    along_x = (at(y, 1 - x, core), at(y, 1 - x, 1 - core))
    along_y = (at(1 - y, x, core), at(1 - y, x, 1 - core))
    near = (partner,) + along_x + along_y
    line = [(k, (z + 1 + k) % n_local, (z + last - k) % n_local) for k in range(last)]

    barrier = pltpu.get_barrier_semaphore()
    for to in near:
        pl.semaphore_signal(barrier, inc=1, device_id=(to, z), device_id_type=MESH)
    for _, to, _ in line:
        pl.semaphore_signal(barrier, inc=1, device_id=(node, to), device_id_type=MESH)

    pl.semaphore_wait(barrier, len(near) + len(line))

    def send(src, dst, send_sem, recv_sem, to_node, to_local):
        return pltpu.make_async_remote_copy(
            src_ref=src, dst_ref=dst, send_sem=send_sem, recv_sem=recv_sem,
            device_id=(to_node, to_local), device_id_type=MESH)

    def cot_copy(i, source, slot, to):
        return send(source, cot_in.at[:, slot * tok : (slot + 1) * tok],
                    cot_send.at[i], cot_recv.at[i], to, z)

    cot_copies = [
        cot_copy(i, cot_t, slot, to)
        for i, (to, slot) in enumerate(((along_x[0], 0), (along_y[0], 4), (partner, 3)))
    ]
    cot_passes = [
        cot_copy(3 + i, cot_in.at[:, slot * tok : (slot + 1) * tok], slot + 1, partner)
        for i, slot in enumerate((0, 4))
    ]

    def column_of(k, owner):
        return pl.ds(aligned(owner * n_local + (z + 1 + k) % n_local, share), share)

    def second_of(k, owner_y, owner_x, owner_core):
        if k % 2 == 0:
            return at(1 - owner_y, owner_x, owner_core)
        return at(owner_y, 1 - owner_x, owner_core)

    def act_copies(k):
        over_x = k % 2 == 0
        first = (y, 1 - x) if over_x else (1 - y, x)
        own_row, first_row = (2, 0) if over_x else (0, 2)
        copies = []
        for i, (to_y, to_x, to_core, row) in enumerate((
            (first[0], first[1], core, first_row),
            (first[0], first[1], 1 - core, first_row + 1),
            (y, x, 1 - core, own_row + 1),
        )):
            to = at(to_y, to_x, to_core)
            for which, owner in ((1, second_of(k, to_y, to_x, to_core)), (0, to)):
                copies.append(send(
                    (act_hbm if k < 2 else act).at[:, column_of(k, owner)],
                    act_in.at[k, row * tok : (row + 1) * tok, which * share : (which + 1) * share],
                    act_send.at[k, 2 * i + which], act_recv.at[k, 2 * i + which], to, z))
        return copies

    def sum_copy(k):
        return send(other_out.at[k], other_in.at[k], s_send.at[k], s_recv.at[k],
                    second_of(k, y, x, core), z)

    def term_copy(k, to):
        return send(term_out.at[k], term_in.at[k], g_send.at[k], g_recv.at[k], node, to)

    parity = (x + y) % 2

    def part_of(of_parity, of_core, begin, size):
        return pl.ds(aligned((of_parity * 2 + of_core) * 2 + begin, eighth), size * eighth)

    def line_copy(k, to):
        part = part_of(parity, core, 0, 2)
        return send(weight.at[part], weight_in.at[k, part], w_send.at[0, k], w_recv.at[0, k], node, to)

    def plane_copies(k, of_parity):
        return [
            send(weight_in.at[k, part], weight_in.at[k, part],
                 w_send.at[1 + i, k], w_recv.at[1 + i, k], to, z)
            for i, (to, part) in enumerate((
                (along_x[0], part_of(of_parity, core, 0, 1)),
                (along_y[0], part_of(of_parity, core, 1, 1))))
        ]

    def pass_copy(k, i, of_parity, of_core):
        part = part_of(of_parity, of_core, 0, 2)
        return send(weight_in.at[k, part], weight_in.at[k, part],
                    w_send.at[3 + i, k], w_recv.at[3 + i, k], partner, z)

    for copy in act_copies(0):
        copy.start()
    loads[2].wait()
    cot_t[...] = cot_ref[...].T
    for copy in cot_copies:
        copy.start()
    loads[0].wait()
    loads[1].wait()
    for b in range(blocks):
        part = codes_ref[b].astype(F32) * scales_ref[b : b + 1, :]
        weight[b * block : (b + 1) * block, :] = part.astype(BF16)
    for k, to, _ in line:
        line_copy(k, to).start()
    for copy in act_copies(1):
        copy.start()
    cot_in[:, 2 * tok : 3 * tok] = cot_t[...]
    loads[3].wait()

    def projected(owner, stored):
        return jnp.dot(act[:, pl.ds(aligned(owner, rows), rows)], stored, preferred_element_type=F32)

    total[...] = projected(z, weight[...])

    def group_term(k):
        over_x = k % 2 == 0
        own_row = 2 if over_x else 0
        own = slice(own_row * tok, (own_row + 1) * tok)
        act_in[k, own, share : 2 * share] = act[:, column_of(k, second_of(k, y, x, core))]
        act_in[k, own, 0:share] = act[:, column_of(k, node)]
        if k == 0:
            for i, copy in enumerate(cot_copies):
                copy.wait_recv()
                if i < 2:
                    cot_passes[i].start()
            if n_local > 2:
                for copy in act_copies(2):
                    copy.start()
        for copy in act_copies(k):
            copy.wait_recv()
        if k == 0:
            for copy in cot_passes:
                copy.wait_recv()
        cot = cot_in[:, 0 : 4 * tok] if over_x else cot_in[:, 2 * tok : 6 * tok]
        both = jnp.dot(cot, act_in[k], preferred_element_type=F32)
        other_out[k] = both[:, share:]
        sum_copy(k).start()
        if k + 3 < n_local:
            for copy in act_copies(k + 3):
                copy.start()
        term_out[k] = both[:, :share]

    def finish_term(k):
        sum_copy(k).wait_recv()
        term_out[k] += other_in[k]
        if k < last:
            term_copy(k, line[k][1]).start()

    early = min(2, n_local)
    for k in range(early):
        group_term(k)
    for k, to, _ in line:
        line_copy(k, to).wait_recv()
        for copy in plane_copies(k, parity):
            copy.start()
        pass_copy(k, 0, parity, core).start()
    for k in range(early):
        finish_term(k)
    for k in range(early, n_local):
        group_term(k)
    for k, _, _ in line:
        for copy in plane_copies(k, 1 - parity):
            copy.wait_recv()
        pass_copy(k, 1, 1 - parity, core).start()
    for k in range(early, n_local):
        finish_term(k)
    for k, _, owner in line:
        pass_copy(k, 0, parity, 1 - core).wait_recv()
        pass_copy(k, 1, 1 - parity, 1 - core).wait_recv()
    def add_owner(k, _):
        total[...] += projected(lax.rem(z + last - k, n_local), weight_in[k])
        return 0

    lax.fori_loop(0, last, add_owner, 0)
    values_ref[...] = total[...].astype(BF16)
    grad = term_out[last]
    for k, to, _ in line:
        term_copy(k, to).wait_recv()
        grad += term_in[k]
    grad_ref[...] = grad.T * norm

    for copy in cot_copies + cot_passes:
        copy.wait_send()
    for k in range(n_local):
        for copy in act_copies(k):
            copy.wait_send()
        sum_copy(k).wait_send()
    for k, to, _ in line:
        line_copy(k, to).wait_send()
        for copy in plane_copies(k, parity):
            copy.wait_send()
        pass_copy(k, 0, parity, core).wait_send()
        pass_copy(k, 1, 1 - parity, core).wait_send()
        term_copy(k, to).wait_send()


def exchanged(n_node, n_local, activations, codes, scales, cotangent):
    tok, width = activations.shape
    blocks, block, head = codes.shape
    rows = blocks * block
    share = width // (n_node * n_local)
    dma = pltpu.SemaphoreType.DMA
    vmem = pl.BlockSpec(memory_space=pltpu.VMEM)
    norm = float(tok * n_node * n_local) ** (-0.5)
    piece = pltpu.VMEM((n_local, head, share), F32)
    return pl.pallas_call(
        functools.partial(exchange_kernel, n_local, norm),
        out_shape=(
            jax.ShapeDtypeStruct((tok, head), BF16),
            jax.ShapeDtypeStruct((share, head), F32),
        ),
        in_specs=[pl.BlockSpec(memory_space=pltpu.HBM)] * 4,
        out_specs=(vmem, vmem),
        scratch_shapes=[
            pltpu.VMEM((tok, width), BF16),
            pltpu.VMEM(codes.shape, BF16),
            pltpu.VMEM(scales.shape, F32),
            pltpu.VMEM(cotangent.shape, BF16),
            pltpu.VMEM((rows, head), BF16),
            pltpu.VMEM((n_local - 1, rows, head), BF16),
            pltpu.VMEM((n_local, 4 * tok, 2 * share), BF16),
            pltpu.VMEM((head, tok), BF16),
            pltpu.VMEM((head, 6 * tok), BF16),
            piece, piece, piece, piece,
            pltpu.VMEM((tok, head), F32),
            dma((4,)), dma((n_local, 6)), dma((n_local, 6)), dma((5,)), dma((5,)),
            dma((5, n_local)), dma((5, n_local)), dma((n_local,)), dma((n_local,)),
            dma((n_local,)), dma((n_local,)),
        ],
        compiler_params=pltpu.CompilerParams(collective_id=0, has_side_effects=True),
        cost_estimate=pl.CostEstimate(
            flops=4 * tok * width * head, bytes_accessed=2 * tok * width, transcendentals=0
        ),
    )(activations, codes, scales, cotangent)


def gathered(n_node, n_local, activations, codes, scales, cotangent):
    head = codes.shape[2]
    stored = (codes.astype(F32) * scales[:, None, :]).astype(BF16).reshape(-1, head)
    weight = lax.all_gather(stored, "local", axis=0, tiled=True)
    values = jnp.dot(activations, weight, preferred_element_type=F32).astype(BF16)
    term = lax.dot_general(
        activations, cotangent, (((0,), (0,)), ((), ())), preferred_element_type=F32
    )
    tokens = activations.shape[0] * n_node * n_local
    term = term * float(tokens) ** (-0.5)
    share = term.shape[0] // (n_node * n_local)
    term = term.reshape(n_node, n_local, share, head)
    term = lax.psum_scatter(term, "local", scatter_dimension=1, tiled=True)
    term = lax.psum_scatter(term, "node", scatter_dimension=0, tiled=True)
    return values, term.reshape(share, head)


def solution(mesh):
    n_node, n_local = mesh.shape["node"], mesh.shape["local"]

    def on_device(activations, codes, scales, cotangent):
        share = activations.shape[1] // (n_node * n_local)
        rows = codes.shape[0] * codes.shape[1]
        tok = activations.shape[0]
        fits = n_node == 8 and n_local > 1 and share % 128 == 0 and rows % 128 == 0 and tok % 128 == 0
        run = exchanged if fits else gathered
        return run(n_node, n_local, activations, codes, scales, cotangent)

    return jax.shard_map(
        on_device,
        mesh=mesh,
        in_specs=(
            P(("node", "local"), None),
            P("local", None, None),
            P("local", None),
            P(("node", "local"), None),
        ),
        out_specs=(P(("node", "local"), None), P(("node", "local"), None)),
        check_vma=False,
    )
```

```python
import functools

import jax
import jax.numpy as jnp
from jax import lax
from jax.experimental import pallas as pl
from jax.experimental.pallas import tpu as pltpu
from jax.sharding import PartitionSpec as P

MESH = pl.DeviceIdType.MESH
F32 = jnp.float32
BF16 = jnp.bfloat16


def aligned(value, unit):
    return pl.multiple_of(value * unit, unit)


def exchange_kernel(
    n_local, norm,
    act_hbm, codes_hbm, scales_hbm, cot_hbm,
    values_ref, grad_ref,
    act, codes_ref, scales_ref, cot_ref, weight, weight_in, act_in, cot_t, cot_in,
    other_out, other_in, term_out, term_in, total,
    load_sem, act_send, act_recv, cot_send, cot_recv,
    line_send, line_recv, w_send, w_recv, s_send, s_recv, g_send, g_recv,
):
    node, z = lax.axis_index("node"), lax.axis_index("local")
    y, x, core = node // 4, (node // 2) % 2, node % 2
    tok = act.shape[0]
    share = grad_ref.shape[0]
    blocks, block, _ = codes_ref.shape
    rows = blocks * block
    quarter = rows // 4
    eighth = quarter // 2
    last = n_local - 1

    loads = [
        pltpu.make_async_copy(there, here, load_sem.at[i])
        for i, (there, here) in enumerate((
            (codes_hbm, codes_ref), (scales_hbm, scales_ref),
            (cot_hbm, cot_ref), (act_hbm, act)))
    ]
    for load in loads:
        load.start()

    def at(to_y, to_x, to_core):
        return (to_y * 2 + to_x) * 2 + to_core

    partner = at(y, x, 1 - core)
    along_x = (at(y, 1 - x, core), at(y, 1 - x, 1 - core))
    along_y = (at(1 - y, x, core), at(1 - y, x, 1 - core))
    near = (partner,) + along_x + along_y
    line = [(k, (z + 1 + k) % n_local, (z + last - k) % n_local) for k in range(last)]

    barrier = pltpu.get_barrier_semaphore()
    for to in near:
        pl.semaphore_signal(barrier, inc=1, device_id=(to, z), device_id_type=MESH)
    for _, to, _ in line:
        pl.semaphore_signal(barrier, inc=1, device_id=(node, to), device_id_type=MESH)

    pl.semaphore_wait(barrier, len(near) + len(line))

    def send(src, dst, send_sem, recv_sem, to_node, to_local):
        return pltpu.make_async_remote_copy(
            src_ref=src, dst_ref=dst, send_sem=send_sem, recv_sem=recv_sem,
            device_id=(to_node, to_local), device_id_type=MESH)

    def cot_copy(i, source, slot, to):
        return send(source, cot_in.at[:, slot * tok : (slot + 1) * tok],
                    cot_send.at[i], cot_recv.at[i], to, z)

    cot_copies = [
        cot_copy(i, cot_t, slot, to)
        for i, (to, slot) in enumerate(((along_x[0], 0), (along_y[0], 4), (partner, 3)))
    ]
    cot_passes = [
        cot_copy(3 + i, cot_in.at[:, slot * tok : (slot + 1) * tok], slot + 1, partner)
        for i, slot in enumerate((0, 4))
    ]

    def column_of(k, owner):
        return pl.ds(aligned(owner * n_local + (z + 1 + k) % n_local, share), share)

    def second_of(k, owner_y, owner_x, owner_core):
        if k % 2 == 0:
            return at(1 - owner_y, owner_x, owner_core)
        return at(owner_y, 1 - owner_x, owner_core)

    def act_copies(k):
        over_x = k % 2 == 0
        first = (y, 1 - x) if over_x else (1 - y, x)
        own_row, first_row = (2, 0) if over_x else (0, 2)
        copies = []
        for i, (to_y, to_x, to_core, row) in enumerate((
            (first[0], first[1], core, first_row),
            (first[0], first[1], 1 - core, first_row + 1),
            (y, x, 1 - core, own_row + 1),
        )):
            to = at(to_y, to_x, to_core)
            for which, owner in ((1, second_of(k, to_y, to_x, to_core)), (0, to)):
                copies.append(send(
                    (act_hbm if k < 2 else act).at[:, column_of(k, owner)],
                    act_in.at[k, row * tok : (row + 1) * tok, which * share : (which + 1) * share],
                    act_send.at[k], act_recv.at[k], to, z))
        return copies

    def act_whole(k):
        ref = act_in.at[k, 0 : 3 * tok]
        return send(ref, ref, act_send.at[k], act_recv.at[k], partner, z)

    def sum_copy(k):
        return send(other_out.at[k], other_in.at[k], s_send.at[k], s_recv.at[k],
                    second_of(k, y, x, core), z)

    def term_copy(k, to):
        return send(term_out.at[k], term_in.at[k], g_send.at[k], g_recv.at[k], node, to)

    parity = (x + y) % 2

    def part_of(of_parity, of_core, begin, size):
        return pl.ds(aligned((of_parity * 2 + of_core) * 2 + begin, eighth), size * eighth)

    def line_copy(k, to):
        part = part_of(parity, core, 0, 2)
        return send(weight.at[part], weight_in.at[k, part], line_send, line_recv, node, to)

    def line_whole():
        ref = weight_in.at[:, part_of(parity, core, 0, 2)]
        return send(ref, ref, line_send, line_recv, partner, z)

    def owners_copy(i, to, part):
        ref = weight_in.at[:, part]
        return send(ref, ref, w_send.at[i], w_recv.at[i], to, z)

    def plane_copies(of_parity):
        return [
            owners_copy(0, along_x[0], part_of(of_parity, core, 0, 1)),
            owners_copy(1, along_y[0], part_of(of_parity, core, 1, 1)),
        ]

    def pass_copy(i, of_parity, of_core):
        return owners_copy(2 + i, partner, part_of(of_parity, of_core, 0, 2))

    for copy in act_copies(0):
        copy.start()
    loads[2].wait()
    cot_t[...] = cot_ref[...].T
    for copy in cot_copies:
        copy.start()
    loads[0].wait()
    loads[1].wait()
    for b in range(blocks):
        part = codes_ref[b].astype(F32) * scales_ref[b : b + 1, :]
        weight[b * block : (b + 1) * block, :] = part.astype(BF16)
    for k, to, _ in line:
        line_copy(k, to).start()
    for copy in act_copies(1):
        copy.start()
    cot_in[:, 2 * tok : 3 * tok] = cot_t[...]
    loads[3].wait()

    def projected(owner, stored):
        return jnp.dot(act[:, pl.ds(aligned(owner, rows), rows)], stored, preferred_element_type=F32)

    total[...] = projected(z, weight[...])

    def group_term(k):
        over_x = k % 2 == 0
        own_row = 2 if over_x else 0
        own = slice(own_row * tok, (own_row + 1) * tok)
        act_in[k, own, share : 2 * share] = act[:, column_of(k, second_of(k, y, x, core))]
        act_in[k, own, 0:share] = act[:, column_of(k, node)]
        if k == 0:
            for i, copy in enumerate(cot_copies):
                copy.wait_recv()
                if i < 2:
                    cot_passes[i].start()
            if n_local > 2:
                for copy in act_copies(2):
                    copy.start()
        act_whole(k).wait_recv()
        if k == 0:
            for copy in cot_passes:
                copy.wait_recv()
        cot = cot_in[:, 0 : 4 * tok] if over_x else cot_in[:, 2 * tok : 6 * tok]
        both = jnp.dot(cot, act_in[k], preferred_element_type=F32)
        other_out[k] = both[:, share:]
        sum_copy(k).start()
        if k + 3 < n_local:
            for copy in act_copies(k + 3):
                copy.start()
        term_out[k] = both[:, :share]

    def finish_term(k):
        sum_copy(k).wait_recv()
        term_out[k] += other_in[k]
        if k < last:
            term_copy(k, line[k][1]).start()

    def add_owner(k, _):
        total[...] += projected(lax.rem(z + last - k, n_local), weight_in[k])
        return 0

    for k in range(n_local):
        group_term(k)
        if k == 0:
            line_whole().wait_recv()
            for copy in plane_copies(parity):
                copy.start()
            pass_copy(0, parity, core).start()
        else:
            finish_term(k - 1)
    for copy in plane_copies(1 - parity):
        copy.wait_recv()
    pass_copy(1, 1 - parity, core).start()
    for copy in cot_copies + cot_passes + plane_copies(parity):
        copy.wait_send()
    for k in range(n_local):
        act_whole(k).wait_send()
    line_whole().wait_send()
    pass_copy(0, parity, core).wait_send()
    pass_copy(0, parity, 1 - core).wait_recv()
    pass_copy(1, 1 - parity, 1 - core).wait_recv()
    lax.fori_loop(0, last, add_owner, 0)
    values_ref[...] = total[...].astype(BF16)
    finish_term(last)
    pass_copy(1, 1 - parity, core).wait_send()
    for k in range(n_local):
        sum_copy(k).wait_send()
    grad = term_out[last]
    for k, to, _ in line:
        term_copy(k, to).wait_recv()
        grad += term_in[k]
    grad_ref[...] = grad.T * norm
    for k, to, _ in line:
        term_copy(k, to).wait_send()


def exchanged(n_node, n_local, activations, codes, scales, cotangent):
    tok, width = activations.shape
    blocks, block, head = codes.shape
    rows = blocks * block
    share = width // (n_node * n_local)
    dma = pltpu.SemaphoreType.DMA
    vmem = pl.BlockSpec(memory_space=pltpu.VMEM)
    norm = float(tok * n_node * n_local) ** (-0.5)
    piece = pltpu.VMEM((n_local, head, share), F32)
    return pl.pallas_call(
        functools.partial(exchange_kernel, n_local, norm),
        out_shape=(
            jax.ShapeDtypeStruct((tok, head), BF16),
            jax.ShapeDtypeStruct((share, head), F32),
        ),
        in_specs=[pl.BlockSpec(memory_space=pltpu.HBM)] * 4,
        out_specs=(vmem, vmem),
        scratch_shapes=[
            pltpu.VMEM((tok, width), BF16),
            pltpu.VMEM(codes.shape, BF16),
            pltpu.VMEM(scales.shape, F32),
            pltpu.VMEM(cotangent.shape, BF16),
            pltpu.VMEM((rows, head), BF16),
            pltpu.VMEM((n_local - 1, rows, head), BF16),
            pltpu.VMEM((n_local, 4 * tok, 2 * share), BF16),
            pltpu.VMEM((head, tok), BF16),
            pltpu.VMEM((head, 6 * tok), BF16),
            piece, piece, piece, piece,
            pltpu.VMEM((tok, head), F32),
            dma((4,)), dma((n_local,)), dma((n_local,)), dma((5,)), dma((5,)),
            dma, dma, dma((4,)), dma((4,)), dma((n_local,)), dma((n_local,)),
            dma((n_local,)), dma((n_local,)),
        ],
        compiler_params=pltpu.CompilerParams(collective_id=0, has_side_effects=True),
        cost_estimate=pl.CostEstimate(
            flops=4 * tok * width * head, bytes_accessed=2 * tok * width, transcendentals=0
        ),
    )(activations, codes, scales, cotangent)


def gathered(n_node, n_local, activations, codes, scales, cotangent):
    head = codes.shape[2]
    stored = (codes.astype(F32) * scales[:, None, :]).astype(BF16).reshape(-1, head)
    weight = lax.all_gather(stored, "local", axis=0, tiled=True)
    values = jnp.dot(activations, weight, preferred_element_type=F32).astype(BF16)
    term = lax.dot_general(
        activations, cotangent, (((0,), (0,)), ((), ())), preferred_element_type=F32
    )
    tokens = activations.shape[0] * n_node * n_local
    term = term * float(tokens) ** (-0.5)
    share = term.shape[0] // (n_node * n_local)
    term = term.reshape(n_node, n_local, share, head)
    term = lax.psum_scatter(term, "local", scatter_dimension=1, tiled=True)
    term = lax.psum_scatter(term, "node", scatter_dimension=0, tiled=True)
    return values, term.reshape(share, head)


def solution(mesh):
    n_node, n_local = mesh.shape["node"], mesh.shape["local"]

    def on_device(activations, codes, scales, cotangent):
        share = activations.shape[1] // (n_node * n_local)
        rows = codes.shape[0] * codes.shape[1]
        tok = activations.shape[0]
        fits = n_node == 8 and n_local > 1 and share % 128 == 0 and rows % 128 == 0 and tok % 128 == 0
        run = exchanged if fits else gathered
        return run(n_node, n_local, activations, codes, scales, cotangent)

    return jax.shard_map(
        on_device,
        mesh=mesh,
        in_specs=(
            P(("node", "local"), None),
            P("local", None, None),
            P("local", None),
            P(("node", "local"), None),
        ),
        out_specs=(P(("node", "local"), None), P(("node", "local"), None)),
        check_vma=False,
    )
```

```python
import functools

import jax
import jax.numpy as jnp
from jax import lax
from jax.experimental import pallas as pl
from jax.experimental.pallas import tpu as pltpu
from jax.sharding import PartitionSpec as P

MESH = pl.DeviceIdType.MESH
F32 = jnp.float32
BF16 = jnp.bfloat16


def aligned(value, unit):
    return pl.multiple_of(value * unit, unit)


def exchange_kernel(
    n_local, norm,
    act_hbm, codes_hbm, scales_hbm, cot_hbm,
    values_ref, grad_ref,
    act, act_parts, codes_ref, scales_ref, cot_ref, weight, weight_in, act_in, cot_t, cot_in,
    other_out, other_in, term_out, term_in, total,
    load_sem, act_send, act_recv, cot_send, cot_recv,
    line_send, line_recv, w_send, w_recv, s_send, s_recv, g_send, g_recv,
):
    node, z = lax.axis_index("node"), lax.axis_index("local")
    y, x, core = node // 4, (node // 2) % 2, node % 2
    tok = act.shape[0]
    share = grad_ref.shape[0]
    blocks, block, _ = codes_ref.shape
    rows = blocks * block
    quarter = rows // 4
    eighth = quarter // 2
    last = n_local - 1

    loads = [
        pltpu.make_async_copy(there, here, load_sem.at[i])
        for i, (there, here) in enumerate((
            (codes_hbm, codes_ref), (scales_hbm, scales_ref),
            (cot_hbm, cot_ref), (act_hbm, act)))
    ]
    for load in loads:
        load.start()

    def at(to_y, to_x, to_core):
        return (to_y * 2 + to_x) * 2 + to_core

    partner = at(y, x, 1 - core)
    along_x = (at(y, 1 - x, core), at(y, 1 - x, 1 - core))
    along_y = (at(1 - y, x, core), at(1 - y, x, 1 - core))
    near = (partner,) + along_x + along_y
    line = [(k, (z + 1 + k) % n_local, (z + last - k) % n_local) for k in range(last)]

    barrier = pltpu.get_barrier_semaphore()
    for to in near:
        pl.semaphore_signal(barrier, inc=1, device_id=(to, z), device_id_type=MESH)
    for _, to, _ in line:
        pl.semaphore_signal(barrier, inc=1, device_id=(node, to), device_id_type=MESH)

    pl.semaphore_wait(barrier, len(near) + len(line))

    def send(src, dst, send_sem, recv_sem, to_node, to_local):
        return pltpu.make_async_remote_copy(
            src_ref=src, dst_ref=dst, send_sem=send_sem, recv_sem=recv_sem,
            device_id=(to_node, to_local), device_id_type=MESH)

    def cot_copy(i, source, slot, to):
        return send(source, cot_in.at[slot],
                    cot_send.at[i], cot_recv.at[i], to, z)

    cot_copies = [
        cot_copy(i, cot_t, slot, to)
        for i, (to, slot) in enumerate(((along_x[0], 0), (along_y[0], 4), (partner, 3)))
    ]
    cot_passes = [
        cot_copy(3 + i, cot_in.at[slot], slot + 1, partner)
        for i, slot in enumerate((0, 4))
    ]

    def second_of(k):
        return at(1 - y, x, core) if k % 2 == 0 else at(y, 1 - x, core)

    def chunks_of(k, to_y, to_x, to_core):
        owner = (z + 1 + k) % n_local
        if k % 2 == 0:
            return act_parts.at[:, to_x, to_core, owner]
        return act_parts.at[to_y, :, to_core, owner]

    def act_copies(k):
        over_x = k % 2 == 0
        first = (y, 1 - x) if over_x else (1 - y, x)
        own_row, first_row = (2, 0) if over_x else (0, 2)
        return [
            send(chunks_of(k, to_y, to_x, to_core),
                 act_in.at[k, :, row * tok : (row + 1) * tok],
                 act_send.at[k], act_recv.at[k], at(to_y, to_x, to_core), z)
            for to_y, to_x, to_core, row in (
                (first[0], first[1], core, first_row),
                (first[0], first[1], 1 - core, first_row + 1),
                (y, x, 1 - core, own_row + 1))
        ]

    def act_whole(k):
        ref = act_in.at[k, :, 0 : 3 * tok]
        return send(ref, ref, act_send.at[k], act_recv.at[k], partner, z)

    def sum_copy(k):
        return send(other_out.at[k], other_in.at[k], s_send.at[k], s_recv.at[k],
                    second_of(k), z)

    def term_copy(k, to):
        return send(term_out.at[k], term_in.at[k], g_send.at[k], g_recv.at[k], node, to)

    parity = (x + y) % 2

    def part_of(of_parity, of_core, begin, size):
        return pl.ds(aligned((of_parity * 2 + of_core) * 2 + begin, eighth), size * eighth)

    def line_copy(k, to):
        part = part_of(parity, core, 0, 2)
        return send(weight.at[part], weight_in.at[k, part], line_send, line_recv, node, to)

    def line_whole():
        ref = weight_in.at[:, part_of(parity, core, 0, 2)]
        return send(ref, ref, line_send, line_recv, partner, z)

    def owners_copy(i, to, part):
        ref = weight_in.at[:, part]
        return send(ref, ref, w_send.at[i], w_recv.at[i], to, z)

    def plane_copies(of_parity):
        return [
            owners_copy(0, along_x[0], part_of(of_parity, core, 0, 1)),
            owners_copy(1, along_y[0], part_of(of_parity, core, 1, 1)),
        ]

    def pass_copy(i, of_parity, of_core):
        return owners_copy(2 + i, partner, part_of(of_parity, of_core, 0, 2))

    loads[3].wait()
    for i in range(8):
        for j in range(n_local):
            column = (i * n_local + j) * share
            act_parts[i // 4, (i // 2) % 2, i % 2, j] = act[:, column : column + share]
    for copy in act_copies(0):
        copy.start()
    loads[2].wait()
    cot_t[...] = cot_ref[...].T
    for copy in cot_copies:
        copy.start()
    loads[0].wait()
    loads[1].wait()
    for b in range(blocks):
        part = codes_ref[b].astype(F32) * scales_ref[b : b + 1, :]
        weight[b * block : (b + 1) * block, :] = part.astype(BF16)
    for k, to, _ in line:
        line_copy(k, to).start()
    for copy in act_copies(1):
        copy.start()
    cot_in[2] = cot_t[...]

    def projected(owner, stored):
        return jnp.dot(act[:, pl.ds(aligned(owner, rows), rows)], stored, preferred_element_type=F32)

    total[...] = projected(z, weight[...])

    def group_term(k):
        over_x = k % 2 == 0
        own_row = 2 if over_x else 0
        own = slice(own_row * tok, (own_row + 1) * tok)
        act_in[k, :, own, :] = chunks_of(k, y, x, core)[...]
        if k == 0:
            for i, copy in enumerate(cot_copies):
                copy.wait_recv()
                if i < 2:
                    cot_passes[i].start()
            if n_local > 2:
                for copy in act_copies(2):
                    copy.start()
        act_whole(k).wait_recv()
        if k == 0:
            for copy in cot_passes:
                copy.wait_recv()
        begin = 0 if over_x else 2
        mine = y if over_x else x
        cot = jnp.concatenate([cot_in[begin + i] for i in range(4)], axis=1)
        other_out[k] = jnp.dot(cot, act_in[k, 1 - mine], preferred_element_type=F32)
        sum_copy(k).start()
        if k + 3 < n_local:
            for copy in act_copies(k + 3):
                copy.start()
        term_out[k] = jnp.dot(cot, act_in[k, mine], preferred_element_type=F32)

    def finish_term(k):
        sum_copy(k).wait_recv()
        term_out[k] += other_in[k]
        if k < last:
            term_copy(k, line[k][1]).start()

    def add_owner(k, _):
        total[...] += projected(lax.rem(z + last - k, n_local), weight_in[k])
        return 0

    for k in range(n_local):
        group_term(k)
        if k == 0:
            line_whole().wait_recv()
            for copy in plane_copies(parity):
                copy.start()
            pass_copy(0, parity, core).start()
        else:
            finish_term(k - 1)
    for copy in plane_copies(1 - parity):
        copy.wait_recv()
    pass_copy(1, 1 - parity, core).start()
    for copy in cot_copies + cot_passes + plane_copies(parity):
        copy.wait_send()
    for k in range(n_local):
        act_whole(k).wait_send()
    line_whole().wait_send()
    pass_copy(0, parity, core).wait_send()
    pass_copy(0, parity, 1 - core).wait_recv()
    pass_copy(1, 1 - parity, 1 - core).wait_recv()
    lax.fori_loop(0, last, add_owner, 0)
    values_ref[...] = total[...].astype(BF16)
    finish_term(last)
    pass_copy(1, 1 - parity, core).wait_send()
    for k in range(n_local):
        sum_copy(k).wait_send()
    grad = term_out[last]
    for k, to, _ in line:
        term_copy(k, to).wait_recv()
        grad += term_in[k]
    grad_ref[...] = grad.T * norm
    for k, to, _ in line:
        term_copy(k, to).wait_send()


def exchanged(n_node, n_local, activations, codes, scales, cotangent):
    tok, width = activations.shape
    blocks, block, head = codes.shape
    rows = blocks * block
    share = width // (n_node * n_local)
    dma = pltpu.SemaphoreType.DMA
    vmem = pl.BlockSpec(memory_space=pltpu.VMEM)
    norm = float(tok * n_node * n_local) ** (-0.5)
    piece = pltpu.VMEM((n_local, head, share), F32)
    return pl.pallas_call(
        functools.partial(exchange_kernel, n_local, norm),
        out_shape=(
            jax.ShapeDtypeStruct((tok, head), BF16),
            jax.ShapeDtypeStruct((share, head), F32),
        ),
        in_specs=[pl.BlockSpec(memory_space=pltpu.HBM)] * 4,
        out_specs=(vmem, vmem),
        scratch_shapes=[
            pltpu.VMEM((tok, width), BF16),
            pltpu.VMEM((2, 2, 2, n_local, tok, share), BF16),
            pltpu.VMEM(codes.shape, BF16),
            pltpu.VMEM(scales.shape, F32),
            pltpu.VMEM(cotangent.shape, BF16),
            pltpu.VMEM((rows, head), BF16),
            pltpu.VMEM((n_local - 1, rows, head), BF16),
            pltpu.VMEM((n_local, 2, 4 * tok, share), BF16),
            pltpu.VMEM((head, tok), BF16),
            pltpu.VMEM((6, head, tok), BF16),
            piece, piece, piece, piece,
            pltpu.VMEM((tok, head), F32),
            dma((4,)), dma((n_local,)), dma((n_local,)), dma((5,)), dma((5,)),
            dma, dma, dma((4,)), dma((4,)), dma((n_local,)), dma((n_local,)),
            dma((n_local,)), dma((n_local,)),
        ],
        compiler_params=pltpu.CompilerParams(collective_id=0, has_side_effects=True),
        cost_estimate=pl.CostEstimate(
            flops=4 * tok * width * head, bytes_accessed=2 * tok * width, transcendentals=0
        ),
    )(activations, codes, scales, cotangent)


def gathered(n_node, n_local, activations, codes, scales, cotangent):
    head = codes.shape[2]
    stored = (codes.astype(F32) * scales[:, None, :]).astype(BF16).reshape(-1, head)
    weight = lax.all_gather(stored, "local", axis=0, tiled=True)
    values = jnp.dot(activations, weight, preferred_element_type=F32).astype(BF16)
    term = lax.dot_general(
        activations, cotangent, (((0,), (0,)), ((), ())), preferred_element_type=F32
    )
    tokens = activations.shape[0] * n_node * n_local
    term = term * float(tokens) ** (-0.5)
    share = term.shape[0] // (n_node * n_local)
    term = term.reshape(n_node, n_local, share, head)
    term = lax.psum_scatter(term, "local", scatter_dimension=1, tiled=True)
    term = lax.psum_scatter(term, "node", scatter_dimension=0, tiled=True)
    return values, term.reshape(share, head)


def solution(mesh):
    n_node, n_local = mesh.shape["node"], mesh.shape["local"]

    def on_device(activations, codes, scales, cotangent):
        share = activations.shape[1] // (n_node * n_local)
        rows = codes.shape[0] * codes.shape[1]
        tok = activations.shape[0]
        fits = n_node == 8 and n_local > 1 and share % 128 == 0 and rows % 128 == 0 and tok % 128 == 0
        run = exchanged if fits else gathered
        return run(n_node, n_local, activations, codes, scales, cotangent)

    return jax.shard_map(
        on_device,
        mesh=mesh,
        in_specs=(
            P(("node", "local"), None),
            P("local", None, None),
            P("local", None),
            P(("node", "local"), None),
        ),
        out_specs=(P(("node", "local"), None), P(("node", "local"), None)),
        check_vma=False,
    )
```

```python
import functools

import jax
import jax.numpy as jnp
from jax import lax
from jax.experimental import pallas as pl
from jax.experimental.pallas import tpu as pltpu
from jax.sharding import PartitionSpec as P

MESH = pl.DeviceIdType.MESH
F32 = jnp.float32
BF16 = jnp.bfloat16


def aligned(value, unit):
    return pl.multiple_of(value * unit, unit)


def exchange_kernel(
    n_local, norm,
    act_hbm, codes_hbm, scales_hbm, cot_hbm,
    values_ref, grad_ref,
    act, act_parts, codes_ref, scales_ref, cot_ref, weight, weight_in, act_in, cot_t, cot_in,
    other_out, other_in, term_out, term_in, total,
    load_sem, act_send, act_recv, cot_send, cot_recv,
    line_send, line_recv, w_send, w_recv, s_send, s_recv, g_send, g_recv,
):
    node, z = lax.axis_index("node"), lax.axis_index("local")
    y, x, core = node // 4, (node // 2) % 2, node % 2
    tok = act.shape[0]
    share = grad_ref.shape[0]
    blocks, block, _ = codes_ref.shape
    rows = blocks * block
    quarter = rows // 4
    eighth = quarter // 2
    last = n_local - 1

    loads = [
        pltpu.make_async_copy(there, here, load_sem.at[i])
        for i, (there, here) in enumerate((
            (codes_hbm, codes_ref), (scales_hbm, scales_ref),
            (cot_hbm, cot_ref), (act_hbm, act)))
    ]
    for load in loads:
        load.start()

    def at(to_y, to_x, to_core):
        return (to_y * 2 + to_x) * 2 + to_core

    partner = at(y, x, 1 - core)
    along_x = (at(y, 1 - x, core), at(y, 1 - x, 1 - core))
    along_y = (at(1 - y, x, core), at(1 - y, x, 1 - core))
    near = (partner,) + along_x + along_y
    line = [(k, (z + 1 + k) % n_local, (z + last - k) % n_local) for k in range(last)]

    barrier = pltpu.get_barrier_semaphore()
    for to in near:
        pl.semaphore_signal(barrier, inc=1, device_id=(to, z), device_id_type=MESH)
    for _, to, _ in line:
        pl.semaphore_signal(barrier, inc=1, device_id=(node, to), device_id_type=MESH)

    pl.semaphore_wait(barrier, len(near) + len(line))

    def send(src, dst, send_sem, recv_sem, to_node, to_local):
        return pltpu.make_async_remote_copy(
            src_ref=src, dst_ref=dst, send_sem=send_sem, recv_sem=recv_sem,
            device_id=(to_node, to_local), device_id_type=MESH)

    def cot_copy(i, source, slot, to):
        return send(source, cot_in.at[slot],
                    cot_send.at[i], cot_recv.at[i], to, z)

    cot_copies = [
        cot_copy(i, cot_t, slot, to)
        for i, (to, slot) in enumerate(((along_x[0], 0), (along_y[0], 4), (partner, 3)))
    ]
    cot_passes = [
        cot_copy(3 + i, cot_in.at[slot], slot + 1, partner)
        for i, slot in enumerate((0, 4))
    ]

    def second_of(k):
        return at(1 - y, x, core) if k % 2 == 0 else at(y, 1 - x, core)

    def column_of(k, owner):
        return pl.ds(aligned(owner * n_local + (z + 1 + k) % n_local, share), share)

    def chunks_of(k, to_y, to_x, to_core):
        owner = (z + 1 + k) % n_local
        if k % 2 == 0:
            return act_parts.at[:, to_x, to_core, owner]
        return act_parts.at[to_y, :, to_core, owner]

    def act_copies(k):
        over_x = k % 2 == 0
        first = (y, 1 - x) if over_x else (1 - y, x)
        own_row, first_row = (2, 0) if over_x else (0, 2)
        copies = []
        for to_y, to_x, to_core, row in (
            (first[0], first[1], core, first_row),
            (first[0], first[1], 1 - core, first_row + 1),
            (y, x, 1 - core, own_row + 1),
        ):
            place = pl.ds(row * tok, tok)
            if k < 2:
                pairs = [
                    (act_hbm.at[:, column_of(k, at(i, to_x, to_core) if over_x else at(to_y, i, to_core))],
                     act_in.at[k, i, place])
                    for i in range(2)
                ]
            else:
                pairs = [(chunks_of(k, to_y, to_x, to_core), act_in.at[k, :, place])]
            for src, dst in pairs:
                copies.append(send(src, dst, act_send.at[k], act_recv.at[k],
                                   at(to_y, to_x, to_core), z))
        return copies

    def act_whole(k):
        ref = act_in.at[k, :, 0 : 3 * tok]
        return send(ref, ref, act_send.at[k], act_recv.at[k], partner, z)

    def sum_copy(k):
        return send(other_out.at[k], other_in.at[k], s_send.at[k], s_recv.at[k],
                    second_of(k), z)

    def term_copy(k, to):
        return send(term_out.at[k], term_in.at[k], g_send.at[k], g_recv.at[k], node, to)

    parity = (x + y) % 2

    def part_of(of_parity, of_core, begin, size):
        return pl.ds(aligned((of_parity * 2 + of_core) * 2 + begin, eighth), size * eighth)

    def line_copy(k, to):
        part = part_of(parity, core, 0, 2)
        return send(weight.at[part], weight_in.at[k, part], line_send, line_recv, node, to)

    def line_whole():
        ref = weight_in.at[:, part_of(parity, core, 0, 2)]
        return send(ref, ref, line_send, line_recv, partner, z)

    def owners_copy(i, to, part):
        ref = weight_in.at[:, part]
        return send(ref, ref, w_send.at[i], w_recv.at[i], to, z)

    def plane_copies(of_parity):
        return [
            owners_copy(0, along_x[0], part_of(of_parity, core, 0, 1)),
            owners_copy(1, along_y[0], part_of(of_parity, core, 1, 1)),
        ]

    def pass_copy(i, of_parity, of_core):
        return owners_copy(2 + i, partner, part_of(of_parity, of_core, 0, 2))

    for copy in act_copies(0) + act_copies(1):
        copy.start()
    loads[2].wait()
    cot_t[...] = cot_ref[...].T
    for copy in cot_copies:
        copy.start()
    loads[0].wait()
    loads[1].wait()
    for b in range(blocks):
        part = codes_ref[b].astype(F32) * scales_ref[b : b + 1, :]
        weight[b * block : (b + 1) * block, :] = part.astype(BF16)
    for k, to, _ in line:
        line_copy(k, to).start()
    loads[3].wait()
    for i in range(8):
        for j in range(n_local):
            column = (i * n_local + j) * share
            act_parts[i // 4, (i // 2) % 2, i % 2, j] = act[:, column : column + share]
    cot_in[2] = cot_t[...]

    def projected(owner, stored):
        return jnp.dot(act[:, pl.ds(aligned(owner, rows), rows)], stored, preferred_element_type=F32)

    total[...] = projected(z, weight[...])

    def group_term(k):
        over_x = k % 2 == 0
        own_row = 2 if over_x else 0
        own = slice(own_row * tok, (own_row + 1) * tok)
        act_in[k, :, own, :] = chunks_of(k, y, x, core)[...]
        if k == 0:
            for i, copy in enumerate(cot_copies):
                copy.wait_recv()
                if i < 2:
                    cot_passes[i].start()
            if n_local > 2:
                for copy in act_copies(2):
                    copy.start()
        act_whole(k).wait_recv()
        if k == 0:
            for copy in cot_passes:
                copy.wait_recv()
        begin = 0 if over_x else 2
        mine = y if over_x else x
        cot = jnp.concatenate([cot_in[begin + i] for i in range(4)], axis=1)
        other_out[k] = jnp.dot(cot, act_in[k, 1 - mine], preferred_element_type=F32)
        sum_copy(k).start()
        if k + 3 < n_local:
            for copy in act_copies(k + 3):
                copy.start()
        term_out[k] = jnp.dot(cot, act_in[k, mine], preferred_element_type=F32)

    def finish_term(k):
        sum_copy(k).wait_recv()
        term_out[k] += other_in[k]
        if k < last:
            term_copy(k, line[k][1]).start()

    def add_quarter(of_parity, of_core):
        begin = (of_parity * 2 + of_core) * quarter

        def add_owner(k, _):
            column = aligned(lax.rem(z + last - k, n_local) * (rows // quarter)
                             + of_parity * 2 + of_core, quarter)
            total[...] += jnp.dot(
                act[:, pl.ds(column, quarter)],
                weight_in[k, pl.ds(pl.multiple_of(begin, quarter), quarter)],
                preferred_element_type=F32)
            return 0

        lax.fori_loop(0, last, add_owner, 0)

    group_term(0)
    line_whole().wait_recv()
    for copy in plane_copies(parity):
        copy.start()
    pass_copy(0, parity, core).start()
    add_quarter(parity, core)
    for k in range(1, last):
        group_term(k)
        finish_term(k - 1)
    pass_copy(0, parity, 1 - core).wait_recv()
    add_quarter(parity, 1 - core)
    for copy in plane_copies(1 - parity):
        copy.wait_recv()
    pass_copy(1, 1 - parity, core).start()
    finish_term(last - 1)
    group_term(last)
    add_quarter(1 - parity, core)
    for copy in cot_copies + cot_passes + plane_copies(parity):
        copy.wait_send()
    for k in range(n_local):
        act_whole(k).wait_send()
    line_whole().wait_send()
    pass_copy(0, parity, core).wait_send()
    pass_copy(1, 1 - parity, 1 - core).wait_recv()
    add_quarter(1 - parity, 1 - core)
    values_ref[...] = total[...].astype(BF16)
    finish_term(last)
    pass_copy(1, 1 - parity, core).wait_send()
    for k in range(n_local):
        sum_copy(k).wait_send()
    grad = term_out[last]
    for k, to, _ in line:
        term_copy(k, to).wait_recv()
        grad += term_in[k]
    grad_ref[...] = grad.T * norm
    for k, to, _ in line:
        term_copy(k, to).wait_send()


def exchanged(n_node, n_local, activations, codes, scales, cotangent):
    tok, width = activations.shape
    blocks, block, head = codes.shape
    rows = blocks * block
    share = width // (n_node * n_local)
    dma = pltpu.SemaphoreType.DMA
    vmem = pl.BlockSpec(memory_space=pltpu.VMEM)
    norm = float(tok * n_node * n_local) ** (-0.5)
    piece = pltpu.VMEM((n_local, head, share), F32)
    return pl.pallas_call(
        functools.partial(exchange_kernel, n_local, norm),
        out_shape=(
            jax.ShapeDtypeStruct((tok, head), BF16),
            jax.ShapeDtypeStruct((share, head), F32),
        ),
        in_specs=[pl.BlockSpec(memory_space=pltpu.HBM)] * 4,
        out_specs=(vmem, vmem),
        scratch_shapes=[
            pltpu.VMEM((tok, width), BF16),
            pltpu.VMEM((2, 2, 2, n_local, tok, share), BF16),
            pltpu.VMEM(codes.shape, BF16),
            pltpu.VMEM(scales.shape, F32),
            pltpu.VMEM(cotangent.shape, BF16),
            pltpu.VMEM((rows, head), BF16),
            pltpu.VMEM((n_local - 1, rows, head), BF16),
            pltpu.VMEM((n_local, 2, 4 * tok, share), BF16),
            pltpu.VMEM((head, tok), BF16),
            pltpu.VMEM((6, head, tok), BF16),
            piece, piece, piece, piece,
            pltpu.VMEM((tok, head), F32),
            dma((4,)), dma((n_local,)), dma((n_local,)), dma((5,)), dma((5,)),
            dma, dma, dma((4,)), dma((4,)), dma((n_local,)), dma((n_local,)),
            dma((n_local,)), dma((n_local,)),
        ],
        compiler_params=pltpu.CompilerParams(collective_id=0, has_side_effects=True),
        cost_estimate=pl.CostEstimate(
            flops=4 * tok * width * head, bytes_accessed=2 * tok * width, transcendentals=0
        ),
    )(activations, codes, scales, cotangent)


def gathered(n_node, n_local, activations, codes, scales, cotangent):
    head = codes.shape[2]
    stored = (codes.astype(F32) * scales[:, None, :]).astype(BF16).reshape(-1, head)
    weight = lax.all_gather(stored, "local", axis=0, tiled=True)
    values = jnp.dot(activations, weight, preferred_element_type=F32).astype(BF16)
    term = lax.dot_general(
        activations, cotangent, (((0,), (0,)), ((), ())), preferred_element_type=F32
    )
    tokens = activations.shape[0] * n_node * n_local
    term = term * float(tokens) ** (-0.5)
    share = term.shape[0] // (n_node * n_local)
    term = term.reshape(n_node, n_local, share, head)
    term = lax.psum_scatter(term, "local", scatter_dimension=1, tiled=True)
    term = lax.psum_scatter(term, "node", scatter_dimension=0, tiled=True)
    return values, term.reshape(share, head)


def solution(mesh):
    n_node, n_local = mesh.shape["node"], mesh.shape["local"]

    def on_device(activations, codes, scales, cotangent):
        share = activations.shape[1] // (n_node * n_local)
        rows = codes.shape[0] * codes.shape[1]
        tok = activations.shape[0]
        fits = n_node == 8 and n_local > 1 and share % 128 == 0 and rows % 512 == 0 and tok % 128 == 0
        run = exchanged if fits else gathered
        return run(n_node, n_local, activations, codes, scales, cotangent)

    return jax.shard_map(
        on_device,
        mesh=mesh,
        in_specs=(
            P(("node", "local"), None),
            P("local", None, None),
            P("local", None),
            P(("node", "local"), None),
        ),
        out_specs=(P(("node", "local"), None), P(("node", "local"), None)),
        check_vma=False,
    )
```

```python
import functools

import jax
import jax.numpy as jnp
from jax import lax
from jax.experimental import pallas as pl
from jax.experimental.pallas import tpu as pltpu
from jax.sharding import PartitionSpec as P

MESH = pl.DeviceIdType.MESH
F32 = jnp.float32
BF16 = jnp.bfloat16


def aligned(value, unit):
    return pl.multiple_of(value * unit, unit)


def exchange_kernel(
    n_local, norm,
    act_hbm, codes_hbm, scales_hbm, cot_hbm,
    values_ref, grad_ref,
    act, act_parts, codes_ref, scales_ref, cot_ref, weight, weight_in, act_in, cot_t, cot_in,
    other_out, other_in, term_out, term_in, total,
    load_sem, act_send, act_recv, cot_send, cot_recv,
    w_send, w_recv, f_send, f_recv, s_send, s_recv, g_send, g_recv,
):
    node, z = lax.axis_index("node"), lax.axis_index("local")
    y, x, core = node // 4, (node // 2) % 2, node % 2
    tok = act.shape[0]
    share = grad_ref.shape[0]
    blocks, block, _ = codes_ref.shape
    rows = blocks * block
    half = rows // 2
    last = n_local - 1

    loads = [
        pltpu.make_async_copy(there, here, load_sem.at[i])
        for i, (there, here) in enumerate((
            (codes_hbm, codes_ref), (scales_hbm, scales_ref),
            (cot_hbm, cot_ref), (act_hbm, act)))
    ]
    for load in loads:
        load.start()

    def at(to_y, to_x, to_core):
        return (to_y * 2 + to_x) * 2 + to_core

    partner = at(y, x, 1 - core)
    along_x = (at(y, 1 - x, core), at(y, 1 - x, 1 - core))
    along_y = (at(1 - y, x, core), at(1 - y, x, 1 - core))
    near = (partner,) + along_x + along_y
    line = [(k, (z + 1 + k) % n_local, (z + last - k) % n_local) for k in range(last)]

    barrier = pltpu.get_barrier_semaphore()
    for to in near:
        pl.semaphore_signal(barrier, inc=1, device_id=(to, z), device_id_type=MESH)
    for _, to, _ in line:
        pl.semaphore_signal(barrier, inc=1, device_id=(node, to), device_id_type=MESH)

    pl.semaphore_wait(barrier, len(near) + len(line))

    def send(src, dst, send_sem, recv_sem, to_node, to_local):
        return pltpu.make_async_remote_copy(
            src_ref=src, dst_ref=dst, send_sem=send_sem, recv_sem=recv_sem,
            device_id=(to_node, to_local), device_id_type=MESH)

    def cot_copy(i, source, slot, to):
        return send(source, cot_in.at[slot],
                    cot_send.at[i], cot_recv.at[i], to, z)

    cot_copies = [
        cot_copy(i, cot_t, slot, to)
        for i, (to, slot) in enumerate(((along_x[0], 0), (along_y[0], 4), (partner, 3)))
    ]
    cot_passes = [
        cot_copy(3 + i, cot_in.at[slot], slot + 1, partner)
        for i, slot in enumerate((0, 4))
    ]

    def second_of(k):
        return at(1 - y, x, core) if k % 2 == 0 else at(y, 1 - x, core)

    def column_of(k, owner):
        return pl.ds(aligned(owner * n_local + (z + 1 + k) % n_local, share), share)

    def chunks_of(k, to_y, to_x, to_core):
        owner = (z + 1 + k) % n_local
        if k % 2 == 0:
            return act_parts.at[:, to_x, to_core, owner]
        return act_parts.at[to_y, :, to_core, owner]

    def act_copies(k):
        over_x = k % 2 == 0
        first = (y, 1 - x) if over_x else (1 - y, x)
        own_row, first_row = (2, 0) if over_x else (0, 2)
        copies = []
        for to_y, to_x, to_core, row in (
            (first[0], first[1], core, first_row),
            (first[0], first[1], 1 - core, first_row + 1),
            (y, x, 1 - core, own_row + 1),
        ):
            place = pl.ds(row * tok, tok)
            if k < 2:
                pairs = [
                    (act_hbm.at[:, column_of(k, at(i, to_x, to_core) if over_x else at(to_y, i, to_core))],
                     act_in.at[k, i, place])
                    for i in range(2)
                ]
            else:
                pairs = [(chunks_of(k, to_y, to_x, to_core), act_in.at[k, :, place])]
            for src, dst in pairs:
                copies.append(send(src, dst, act_send.at[k], act_recv.at[k],
                                   at(to_y, to_x, to_core), z))
        return copies

    def act_whole(k):
        ref = act_in.at[k, :, 0 : 3 * tok]
        return send(ref, ref, act_send.at[k], act_recv.at[k], partner, z)

    def sum_copy(k):
        return send(other_out.at[k], other_in.at[k], s_send.at[k], s_recv.at[k],
                    second_of(k), z)

    def term_copy(k, to):
        return send(term_out.at[k], term_in.at[k], g_send.at[k], g_recv.at[k], node, to)

    def half_of(of_core):
        return pl.ds(aligned(of_core, half), half)

    def line_copy(k, to):
        part = half_of(core)
        return send(weight.at[part], weight_in.at[k, part], w_send.at[k], w_recv.at[k], node, to)

    def pass_copy(k, of_core):
        ref = weight_in.at[k, half_of(of_core)]
        return send(ref, ref, f_send.at[k], f_recv.at[k], partner, z)

    for copy in act_copies(0) + act_copies(1):
        copy.start()
    loads[2].wait()
    cot_t[...] = cot_ref[...].T
    for copy in cot_copies:
        copy.start()
    loads[0].wait()
    loads[1].wait()
    for b in range(blocks):
        part = codes_ref[b].astype(F32) * scales_ref[b : b + 1, :]
        weight[b * block : (b + 1) * block, :] = part.astype(BF16)
    for k, to, _ in line:
        line_copy(k, to).start()
    loads[3].wait()
    for i in range(8):
        for j in range(n_local):
            column = (i * n_local + j) * share
            act_parts[i // 4, (i // 2) % 2, i % 2, j] = act[:, column : column + share]
    cot_in[2] = cot_t[...]

    def projected(owner, stored):
        return jnp.dot(act[:, pl.ds(aligned(owner, rows), rows)], stored, preferred_element_type=F32)

    total[...] = projected(z, weight[...])

    def group_term(k):
        over_x = k % 2 == 0
        own_row = 2 if over_x else 0
        own = slice(own_row * tok, (own_row + 1) * tok)
        act_in[k, :, own, :] = chunks_of(k, y, x, core)[...]
        if k == 0:
            for i, copy in enumerate(cot_copies):
                copy.wait_recv()
                if i < 2:
                    cot_passes[i].start()
            if n_local > 2:
                for copy in act_copies(2):
                    copy.start()
        act_whole(k).wait_recv()
        if k == 0:
            for copy in cot_passes:
                copy.wait_recv()
        begin = 0 if over_x else 2
        mine = y if over_x else x
        cot = jnp.concatenate([cot_in[begin + i] for i in range(4)], axis=1)
        other_out[k] = jnp.dot(cot, act_in[k, 1 - mine], preferred_element_type=F32)
        sum_copy(k).start()
        if k + 3 < n_local:
            for copy in act_copies(k + 3):
                copy.start()
        term_out[k] = jnp.dot(cot, act_in[k, mine], preferred_element_type=F32)

    def finish_term(k):
        sum_copy(k).wait_recv()
        term_out[k] += other_in[k]
        if k < last:
            term_copy(k, line[k][1]).start()

    def add_half(k, owner, of_core):
        column = aligned(owner * 2 + of_core, half)
        total[...] += jnp.dot(act[:, pl.ds(column, half)], weight_in[k, half_of(of_core)],
                              preferred_element_type=F32)

    group_term(0)
    for k in range(1, last):
        group_term(k)
        finish_term(k - 1)
    for k, to, owner in line:
        line_copy(k, to).wait_recv()
        pass_copy(k, core).start()
        add_half(k, owner, core)
    finish_term(last - 1)
    group_term(last)
    for copy in cot_copies + cot_passes:
        copy.wait_send()
    for k in range(n_local):
        act_whole(k).wait_send()
    for k, to, owner in line:
        line_copy(k, to).wait_send()
        pass_copy(k, 1 - core).wait_recv()
        add_half(k, owner, 1 - core)
    values_ref[...] = total[...].astype(BF16)
    finish_term(last)
    for k, _, _ in line:
        pass_copy(k, core).wait_send()
    for k in range(n_local):
        sum_copy(k).wait_send()
    grad = term_out[last]
    for k, to, _ in line:
        term_copy(k, to).wait_recv()
        grad += term_in[k]
    grad_ref[...] = grad.T * norm
    for k, to, _ in line:
        term_copy(k, to).wait_send()


def exchanged(n_node, n_local, activations, codes, scales, cotangent):
    tok, width = activations.shape
    blocks, block, head = codes.shape
    rows = blocks * block
    share = width // (n_node * n_local)
    dma = pltpu.SemaphoreType.DMA
    vmem = pl.BlockSpec(memory_space=pltpu.VMEM)
    norm = float(tok * n_node * n_local) ** (-0.5)
    piece = pltpu.VMEM((n_local, head, share), F32)
    return pl.pallas_call(
        functools.partial(exchange_kernel, n_local, norm),
        out_shape=(
            jax.ShapeDtypeStruct((tok, head), BF16),
            jax.ShapeDtypeStruct((share, head), F32),
        ),
        in_specs=[pl.BlockSpec(memory_space=pltpu.HBM)] * 4,
        out_specs=(vmem, vmem),
        scratch_shapes=[
            pltpu.VMEM((tok, width), BF16),
            pltpu.VMEM((2, 2, 2, n_local, tok, share), BF16),
            pltpu.VMEM(codes.shape, BF16),
            pltpu.VMEM(scales.shape, F32),
            pltpu.VMEM(cotangent.shape, BF16),
            pltpu.VMEM((rows, head), BF16),
            pltpu.VMEM((n_local - 1, rows, head), BF16),
            pltpu.VMEM((n_local, 2, 4 * tok, share), BF16),
            pltpu.VMEM((head, tok), BF16),
            pltpu.VMEM((6, head, tok), BF16),
            piece, piece, piece, piece,
            pltpu.VMEM((tok, head), F32),
            dma((4,)), dma((n_local,)), dma((n_local,)), dma((5,)), dma((5,)),
            dma((n_local,)), dma((n_local,)), dma((n_local,)), dma((n_local,)),
            dma((n_local,)), dma((n_local,)),
            dma((n_local,)), dma((n_local,)),
        ],
        compiler_params=pltpu.CompilerParams(collective_id=0, has_side_effects=True),
        cost_estimate=pl.CostEstimate(
            flops=4 * tok * width * head, bytes_accessed=2 * tok * width, transcendentals=0
        ),
    )(activations, codes, scales, cotangent)


def gathered(n_node, n_local, activations, codes, scales, cotangent):
    head = codes.shape[2]
    stored = (codes.astype(F32) * scales[:, None, :]).astype(BF16).reshape(-1, head)
    weight = lax.all_gather(stored, "local", axis=0, tiled=True)
    values = jnp.dot(activations, weight, preferred_element_type=F32).astype(BF16)
    term = lax.dot_general(
        activations, cotangent, (((0,), (0,)), ((), ())), preferred_element_type=F32
    )
    tokens = activations.shape[0] * n_node * n_local
    term = term * float(tokens) ** (-0.5)
    share = term.shape[0] // (n_node * n_local)
    term = term.reshape(n_node, n_local, share, head)
    term = lax.psum_scatter(term, "local", scatter_dimension=1, tiled=True)
    term = lax.psum_scatter(term, "node", scatter_dimension=0, tiled=True)
    return values, term.reshape(share, head)


def solution(mesh):
    n_node, n_local = mesh.shape["node"], mesh.shape["local"]

    def on_device(activations, codes, scales, cotangent):
        share = activations.shape[1] // (n_node * n_local)
        rows = codes.shape[0] * codes.shape[1]
        tok = activations.shape[0]
        fits = n_node == 8 and n_local > 1 and share % 128 == 0 and rows % 256 == 0 and tok % 128 == 0
        run = exchanged if fits else gathered
        return run(n_node, n_local, activations, codes, scales, cotangent)

    return jax.shard_map(
        on_device,
        mesh=mesh,
        in_specs=(
            P(("node", "local"), None),
            P("local", None, None),
            P("local", None),
            P(("node", "local"), None),
        ),
        out_specs=(P(("node", "local"), None), P(("node", "local"), None)),
        check_vma=False,
    )
```

```python
import functools

import jax
import jax.numpy as jnp
from jax import lax
from jax.experimental import pallas as pl
from jax.experimental.pallas import tpu as pltpu
from jax.sharding import PartitionSpec as P

MESH = pl.DeviceIdType.MESH
F32 = jnp.float32
BF16 = jnp.bfloat16


def aligned(value, unit):
    return pl.multiple_of(value * unit, unit)


def exchange_kernel(
    n_local, norm,
    act_hbm, codes_hbm, scales_hbm, cot_hbm,
    values_ref, grad_ref,
    act, act_parts, codes_ref, scales_ref, cot_ref, weight, weight_in, act_in, cot_t, cot_in,
    other_out, other_in, term_out, term_in, total,
    load_sem, act_send, act_recv, cot_send, cot_recv,
    w_send, w_recv, f_send, f_recv, s_send, s_recv, g_send, g_recv,
):
    node, z = lax.axis_index("node"), lax.axis_index("local")
    y, x, core = node // 4, (node // 2) % 2, node % 2
    tok = act.shape[0]
    share = grad_ref.shape[0]
    blocks, block, _ = codes_ref.shape
    rows = blocks * block
    half = rows // 2
    last = n_local - 1

    loads = [
        pltpu.make_async_copy(there, here, load_sem.at[i])
        for i, (there, here) in enumerate((
            (codes_hbm, codes_ref), (scales_hbm, scales_ref),
            (cot_hbm, cot_ref), (act_hbm, act)))
    ]
    for load in loads:
        load.start()

    def at(to_y, to_x, to_core):
        return (to_y * 2 + to_x) * 2 + to_core

    partner = at(y, x, 1 - core)
    along_x = (at(y, 1 - x, core), at(y, 1 - x, 1 - core))
    along_y = (at(1 - y, x, core), at(1 - y, x, 1 - core))
    near = (partner,) + along_x + along_y
    line = [(k, (z + 1 + k) % n_local, (z + last - k) % n_local) for k in range(last)]

    barrier = pltpu.get_barrier_semaphore()
    for to in near:
        pl.semaphore_signal(barrier, inc=1, device_id=(to, z), device_id_type=MESH)
    for _, to, _ in line:
        pl.semaphore_signal(barrier, inc=1, device_id=(node, to), device_id_type=MESH)

    pl.semaphore_wait(barrier, len(near) + len(line))

    def send(src, dst, send_sem, recv_sem, to_node, to_local):
        return pltpu.make_async_remote_copy(
            src_ref=src, dst_ref=dst, send_sem=send_sem, recv_sem=recv_sem,
            device_id=(to_node, to_local), device_id_type=MESH)

    def cot_copy(i, source, slot, to):
        return send(source, cot_in.at[slot],
                    cot_send.at[i], cot_recv.at[i], to, z)

    cot_copies = [
        cot_copy(i, cot_t, slot, to)
        for i, (to, slot) in enumerate(((along_x[0], 0), (along_y[0], 4), (partner, 3)))
    ]
    cot_passes = [
        cot_copy(3 + i, cot_in.at[slot], slot + 1, partner)
        for i, slot in enumerate((0, 4))
    ]

    def second_of(k):
        return at(1 - y, x, core) if k % 2 == 0 else at(y, 1 - x, core)

    def column_of(k, owner):
        return pl.ds(aligned(owner * n_local + (z + 1 + k) % n_local, share), share)

    def chunks_of(k, to_y, to_x, to_core):
        owner = (z + 1 + k) % n_local
        if k % 2 == 0:
            return act_parts.at[:, to_x, to_core, owner]
        return act_parts.at[to_y, :, to_core, owner]

    def act_copies(k):
        over_x = k % 2 == 0
        first = (y, 1 - x) if over_x else (1 - y, x)
        own_row, first_row = (2, 0) if over_x else (0, 2)
        copies = []
        for to_y, to_x, to_core, row in (
            (first[0], first[1], core, first_row),
            (first[0], first[1], 1 - core, first_row + 1),
            (y, x, 1 - core, own_row + 1),
        ):
            place = pl.ds(row * tok, tok)
            if k < 2:
                pairs = [
                    (act_hbm.at[:, column_of(k, at(i, to_x, to_core) if over_x else at(to_y, i, to_core))],
                     act_in.at[k, i, place])
                    for i in range(2)
                ]
            else:
                pairs = [(chunks_of(k, to_y, to_x, to_core), act_in.at[k, :, place])]
            for src, dst in pairs:
                copies.append(send(src, dst, act_send.at[k], act_recv.at[k],
                                   at(to_y, to_x, to_core), z))
        return copies

    def act_whole(k):
        ref = act_in.at[k, :, 0 : 3 * tok]
        return send(ref, ref, act_send.at[k], act_recv.at[k], partner, z)

    def sum_copy(k):
        return send(other_out.at[k], other_in.at[k], s_send.at[k], s_recv.at[k],
                    second_of(k), z)

    def term_copy(k, to):
        return send(term_out.at[k], term_in.at[k], g_send.at[k], g_recv.at[k], node, to)

    def half_of(of_core):
        return pl.ds(aligned(of_core, half), half)

    def line_copy(src, slot, send_sem, to):
        return send(src, weight_in.at[slot, half_of(core)], send_sem, w_recv.at[slot], node, to)

    def line_own(rightward):
        src = weight.at[half_of(core)]
        if rightward:
            return line_copy(src, 0, w_send.at[0], (z + 1) % n_local)
        return line_copy(src, last - 1, w_send.at[1], (z + last) % n_local)

    def line_on(k, rightward):
        src = weight_in.at[k, half_of(core)]
        if rightward:
            return line_copy(src, k + 1, w_send.at[2 + k], (z + 1) % n_local)
        return line_copy(src, k - 1, w_send.at[2 + k], (z + last) % n_local)

    def on_line(act_on):
        pl.when(z < last)(lambda: act_on(line_own(True)))
        pl.when(z > 0)(lambda: act_on(line_own(False)))

    def on_relay(k, act_on):
        if k + 1 < last:
            pl.when((k < z) & (z < last))(lambda: act_on(line_on(k, True)))
        if k > 0:
            pl.when((k >= z) & (z > 0))(lambda: act_on(line_on(k, False)))

    def pass_copy(k, of_core):
        ref = weight_in.at[k, half_of(of_core)]
        return send(ref, ref, f_send.at[k], f_recv.at[k], partner, z)

    for copy in act_copies(0) + act_copies(1):
        copy.start()
    loads[2].wait()
    cot_t[...] = cot_ref[...].T
    for copy in cot_copies:
        copy.start()
    loads[0].wait()
    loads[1].wait()
    for b in range(blocks):
        part = codes_ref[b].astype(F32) * scales_ref[b : b + 1, :]
        weight[b * block : (b + 1) * block, :] = part.astype(BF16)
    on_line(lambda copy: copy.start())
    loads[3].wait()
    for i in range(8):
        for j in range(n_local):
            column = (i * n_local + j) * share
            act_parts[i // 4, (i // 2) % 2, i % 2, j] = act[:, column : column + share]
    cot_in[2] = cot_t[...]

    def projected(owner, stored):
        return jnp.dot(act[:, pl.ds(aligned(owner, rows), rows)], stored, preferred_element_type=F32)

    total[...] = projected(z, weight[...])

    def group_term(k):
        over_x = k % 2 == 0
        own_row = 2 if over_x else 0
        own = slice(own_row * tok, (own_row + 1) * tok)
        act_in[k, :, own, :] = chunks_of(k, y, x, core)[...]
        if k == 0:
            for i, copy in enumerate(cot_copies):
                copy.wait_recv()
                if i < 2:
                    cot_passes[i].start()
            if n_local > 2:
                for copy in act_copies(2):
                    copy.start()
        act_whole(k).wait_recv()
        if k == 0:
            for copy in cot_passes:
                copy.wait_recv()
        begin = 0 if over_x else 2
        mine = y if over_x else x
        cot = jnp.concatenate([cot_in[begin + i] for i in range(4)], axis=1)
        other_out[k] = jnp.dot(cot, act_in[k, 1 - mine], preferred_element_type=F32)
        sum_copy(k).start()
        if k + 3 < n_local:
            for copy in act_copies(k + 3):
                copy.start()
        term_out[k] = jnp.dot(cot, act_in[k, mine], preferred_element_type=F32)

    def finish_term(k):
        sum_copy(k).wait_recv()
        term_out[k] += other_in[k]
        if k < last:
            term_copy(k, line[k][1]).start()

    def add_half(k, owner, of_core):
        column = aligned(owner * 2 + of_core, half)
        total[...] += jnp.dot(act[:, pl.ds(column, half)], weight_in[k, half_of(of_core)],
                              preferred_element_type=F32)

    def relay(distance):
        for k, _, owner in line:
            if min(k, last - 1 - k) == distance:
                line_copy(weight.at[half_of(core)], k, w_send.at[0], (z + 1) % n_local).wait_recv()
                on_relay(k, lambda copy: copy.start())
                pass_copy(k, core).start()
                add_half(k, owner, core)

    for k in range(last):
        group_term(k)
        relay(k)
        if k > 0:
            finish_term(k - 1)
    finish_term(last - 1)
    group_term(last)
    for copy in cot_copies + cot_passes:
        copy.wait_send()
    for k in range(n_local):
        act_whole(k).wait_send()
    on_line(lambda copy: copy.wait_send())
    for k, to, owner in line:
        on_relay(k, lambda copy: copy.wait_send())
        pass_copy(k, 1 - core).wait_recv()
        add_half(k, owner, 1 - core)
    values_ref[...] = total[...].astype(BF16)
    finish_term(last)
    for k, _, _ in line:
        pass_copy(k, core).wait_send()
    for k in range(n_local):
        sum_copy(k).wait_send()
    grad = term_out[last]
    for k, to, _ in line:
        term_copy(k, to).wait_recv()
        grad += term_in[k]
    grad_ref[...] = grad.T * norm
    for k, to, _ in line:
        term_copy(k, to).wait_send()


def exchanged(n_node, n_local, activations, codes, scales, cotangent):
    tok, width = activations.shape
    blocks, block, head = codes.shape
    rows = blocks * block
    share = width // (n_node * n_local)
    dma = pltpu.SemaphoreType.DMA
    vmem = pl.BlockSpec(memory_space=pltpu.VMEM)
    norm = float(tok * n_node * n_local) ** (-0.5)
    piece = pltpu.VMEM((n_local, head, share), F32)
    return pl.pallas_call(
        functools.partial(exchange_kernel, n_local, norm),
        out_shape=(
            jax.ShapeDtypeStruct((tok, head), BF16),
            jax.ShapeDtypeStruct((share, head), F32),
        ),
        in_specs=[pl.BlockSpec(memory_space=pltpu.HBM)] * 4,
        out_specs=(vmem, vmem),
        scratch_shapes=[
            pltpu.VMEM((tok, width), BF16),
            pltpu.VMEM((2, 2, 2, n_local, tok, share), BF16),
            pltpu.VMEM(codes.shape, BF16),
            pltpu.VMEM(scales.shape, F32),
            pltpu.VMEM(cotangent.shape, BF16),
            pltpu.VMEM((rows, head), BF16),
            pltpu.VMEM((n_local - 1, rows, head), BF16),
            pltpu.VMEM((n_local, 2, 4 * tok, share), BF16),
            pltpu.VMEM((head, tok), BF16),
            pltpu.VMEM((6, head, tok), BF16),
            piece, piece, piece, piece,
            pltpu.VMEM((tok, head), F32),
            dma((4,)), dma((n_local,)), dma((n_local,)), dma((5,)), dma((5,)),
            dma((n_local + 1,)), dma((n_local,)), dma((n_local,)), dma((n_local,)),
            dma((n_local,)), dma((n_local,)),
            dma((n_local,)), dma((n_local,)),
        ],
        compiler_params=pltpu.CompilerParams(collective_id=0, has_side_effects=True),
        cost_estimate=pl.CostEstimate(
            flops=4 * tok * width * head, bytes_accessed=2 * tok * width, transcendentals=0
        ),
    )(activations, codes, scales, cotangent)


def gathered(n_node, n_local, activations, codes, scales, cotangent):
    head = codes.shape[2]
    stored = (codes.astype(F32) * scales[:, None, :]).astype(BF16).reshape(-1, head)
    weight = lax.all_gather(stored, "local", axis=0, tiled=True)
    values = jnp.dot(activations, weight, preferred_element_type=F32).astype(BF16)
    term = lax.dot_general(
        activations, cotangent, (((0,), (0,)), ((), ())), preferred_element_type=F32
    )
    tokens = activations.shape[0] * n_node * n_local
    term = term * float(tokens) ** (-0.5)
    share = term.shape[0] // (n_node * n_local)
    term = term.reshape(n_node, n_local, share, head)
    term = lax.psum_scatter(term, "local", scatter_dimension=1, tiled=True)
    term = lax.psum_scatter(term, "node", scatter_dimension=0, tiled=True)
    return values, term.reshape(share, head)


def solution(mesh):
    n_node, n_local = mesh.shape["node"], mesh.shape["local"]

    def on_device(activations, codes, scales, cotangent):
        share = activations.shape[1] // (n_node * n_local)
        rows = codes.shape[0] * codes.shape[1]
        tok = activations.shape[0]
        fits = n_node == 8 and n_local > 1 and share % 128 == 0 and rows % 256 == 0 and tok % 128 == 0
        run = exchanged if fits else gathered
        return run(n_node, n_local, activations, codes, scales, cotangent)

    return jax.shard_map(
        on_device,
        mesh=mesh,
        in_specs=(
            P(("node", "local"), None),
            P("local", None, None),
            P("local", None),
            P(("node", "local"), None),
        ),
        out_specs=(P(("node", "local"), None), P(("node", "local"), None)),
        check_vma=False,
    )
```

```python
import functools

import jax
import jax.numpy as jnp
from jax import lax
from jax.experimental import pallas as pl
from jax.experimental.pallas import tpu as pltpu
from jax.sharding import PartitionSpec as P

MESH = pl.DeviceIdType.MESH
F32 = jnp.float32
BF16 = jnp.bfloat16


def aligned(value, unit):
    return pl.multiple_of(value * unit, unit)


def exchange_kernel(
    n_local, norm,
    act_hbm, codes_hbm, scales_hbm, cot_hbm,
    values_ref, grad_ref,
    act, act_parts, codes_ref, scales_ref, cot_ref, weight, weight_in, act_in, cot_t, cot_in,
    other_out, other_in, term_out, term_in, total,
    load_sem, act_send, act_recv, cot_send, cot_recv,
    w_send, w_recv, f_send, f_recv, s_send, s_recv, g_send, g_recv,
):
    node, z = lax.axis_index("node"), lax.axis_index("local")
    y, x, core = node // 4, (node // 2) % 2, node % 2
    tok = act.shape[0]
    share = grad_ref.shape[0]
    blocks, block, _ = codes_ref.shape
    rows = blocks * block
    half = rows // 2
    last = n_local - 1

    loads = [
        pltpu.make_async_copy(there, here, load_sem.at[i])
        for i, (there, here) in enumerate((
            (codes_hbm, codes_ref), (scales_hbm, scales_ref),
            (cot_hbm, cot_ref), (act_hbm, act)))
    ]
    for load in loads:
        load.start()

    def at(to_y, to_x, to_core):
        return (to_y * 2 + to_x) * 2 + to_core

    partner = at(y, x, 1 - core)
    along_x = (at(y, 1 - x, core), at(y, 1 - x, 1 - core))
    along_y = (at(1 - y, x, core), at(1 - y, x, 1 - core))
    near = (partner,) + along_x + along_y
    line = [(k, (z + 1 + k) % n_local, (z + last - k) % n_local) for k in range(last)]

    barrier = pltpu.get_barrier_semaphore()
    for to in near:
        pl.semaphore_signal(barrier, inc=1, device_id=(to, z), device_id_type=MESH)
    for _, to, _ in line:
        pl.semaphore_signal(barrier, inc=1, device_id=(node, to), device_id_type=MESH)

    pl.semaphore_wait(barrier, len(near) + len(line))

    def send(src, dst, send_sem, recv_sem, to_node, to_local):
        return pltpu.make_async_remote_copy(
            src_ref=src, dst_ref=dst, send_sem=send_sem, recv_sem=recv_sem,
            device_id=(to_node, to_local), device_id_type=MESH)

    def cot_copy(i, source, slot, to):
        return send(source, cot_in.at[slot],
                    cot_send.at[i], cot_recv.at[i], to, z)

    cot_copies = [
        cot_copy(i, cot_t, slot, to)
        for i, (to, slot) in enumerate(((along_x[0], 0), (along_y[0], 4), (partner, 3)))
    ]
    cot_passes = [
        cot_copy(3 + i, cot_in.at[slot], slot + 1, partner)
        for i, slot in enumerate((0, 4))
    ]

    def second_of(k):
        return at(1 - y, x, core) if k % 2 == 0 else at(y, 1 - x, core)

    def column_of(k, owner):
        return pl.ds(aligned(owner * n_local + (z + 1 + k) % n_local, share), share)

    def chunks_of(k, to_y, to_x, to_core):
        owner = (z + 1 + k) % n_local
        if k % 2 == 0:
            return act_parts.at[:, to_x, to_core, owner]
        return act_parts.at[to_y, :, to_core, owner]

    def act_copies(k):
        over_x = k % 2 == 0
        first = (y, 1 - x) if over_x else (1 - y, x)
        own_row, first_row = (2, 0) if over_x else (0, 2)
        copies = []
        for to_y, to_x, to_core, row in (
            (first[0], first[1], core, first_row),
            (first[0], first[1], 1 - core, first_row + 1),
            (y, x, 1 - core, own_row + 1),
        ):
            place = pl.ds(row * tok, tok)
            if k < 2:
                pairs = [
                    (act_hbm.at[:, column_of(k, at(i, to_x, to_core) if over_x else at(to_y, i, to_core))],
                     act_in.at[k, i, place])
                    for i in range(2)
                ]
            else:
                pairs = [(chunks_of(k, to_y, to_x, to_core), act_in.at[k, :, place])]
            for src, dst in pairs:
                copies.append(send(src, dst, act_send.at[k], act_recv.at[k],
                                   at(to_y, to_x, to_core), z))
        return copies

    def act_whole(k):
        ref = act_in.at[k, :, 0 : 3 * tok]
        return send(ref, ref, act_send.at[k], act_recv.at[k], partner, z)

    def sum_copy(k):
        return send(other_out.at[k], other_in.at[k], s_send.at[k], s_recv.at[k],
                    second_of(k), z)

    def term_copy(k, to):
        return send(term_out.at[k], term_in.at[k], g_send.at[k], g_recv.at[k], node, to)

    def half_of(of_core):
        return pl.ds(aligned(of_core, half), half)

    def line_copy(k, to):
        part = half_of(core)
        return send(weight.at[part], weight_in.at[k, part], w_send.at[k], w_recv.at[k], node, to)

    def pass_copy(k, of_core):
        ref = weight_in.at[k, half_of(of_core)]
        return send(ref, ref, f_send.at[k], f_recv.at[k], partner, z)

    for copy in act_copies(0) + act_copies(1):
        copy.start()
    loads[2].wait()
    cot_t[...] = cot_ref[...].T
    for copy in cot_copies:
        copy.start()
    loads[0].wait()
    loads[1].wait()
    for b in range(blocks):
        part = codes_ref[b].astype(F32) * scales_ref[b : b + 1, :]
        weight[b * block : (b + 1) * block, :] = part.astype(BF16)
    for k, to, _ in line:
        line_copy(k, to).start()
    loads[3].wait()
    for i in range(8):
        for j in range(n_local):
            column = (i * n_local + j) * share
            act_parts[i // 4, (i // 2) % 2, i % 2, j] = act[:, column : column + share]
    cot_in[2] = cot_t[...]

    def projected(owner, stored):
        return jnp.dot(act[:, pl.ds(aligned(owner, rows), rows)], stored, preferred_element_type=F32)

    total[...] = projected(z, weight[...])

    def group_term(k):
        over_x = k % 2 == 0
        own_row = 2 if over_x else 0
        own = slice(own_row * tok, (own_row + 1) * tok)
        act_in[k, :, own, :] = chunks_of(k, y, x, core)[...]
        if k == 0:
            for i, copy in enumerate(cot_copies):
                copy.wait_recv()
                if i < 2:
                    cot_passes[i].start()
            for later in range(2, n_local):
                for copy in act_copies(later):
                    copy.start()
        act_whole(k).wait_recv()
        if k == 0:
            for copy in cot_passes:
                copy.wait_recv()
        begin = 0 if over_x else 2
        mine = y if over_x else x
        cot = jnp.concatenate([cot_in[begin + i] for i in range(4)], axis=1)
        other_out[k] = jnp.dot(cot, act_in[k, 1 - mine], preferred_element_type=F32)
        sum_copy(k).start()
        term_out[k] = jnp.dot(cot, act_in[k, mine], preferred_element_type=F32)

    def finish_term(k):
        sum_copy(k).wait_recv()
        term_out[k] += other_in[k]
        if k < last:
            term_copy(k, line[k][1]).start()

    def add_half(k, owner, of_core):
        column = aligned(owner * 2 + of_core, half)
        total[...] += jnp.dot(act[:, pl.ds(column, half)], weight_in[k, half_of(of_core)],
                              preferred_element_type=F32)

    group_term(0)
    for k in range(1, last):
        group_term(k)
        finish_term(k - 1)
        if k == 1:
            for i, to, owner in line:
                line_copy(i, to).wait_recv()
                pass_copy(i, core).start()
                add_half(i, owner, core)
    finish_term(last - 1)
    group_term(last)
    for copy in cot_copies + cot_passes:
        copy.wait_send()
    for k in range(n_local):
        act_whole(k).wait_send()
    for k, to, owner in line:
        line_copy(k, to).wait_send()
        pass_copy(k, 1 - core).wait_recv()
        add_half(k, owner, 1 - core)
    values_ref[...] = total[...].astype(BF16)
    finish_term(last)
    for k, _, _ in line:
        pass_copy(k, core).wait_send()
    for k in range(n_local):
        sum_copy(k).wait_send()
    grad = term_out[last]
    for k, to, _ in line:
        term_copy(k, to).wait_recv()
        grad += term_in[k]
    grad_ref[...] = grad.T * norm
    for k, to, _ in line:
        term_copy(k, to).wait_send()


def exchanged(n_node, n_local, activations, codes, scales, cotangent):
    tok, width = activations.shape
    blocks, block, head = codes.shape
    rows = blocks * block
    share = width // (n_node * n_local)
    dma = pltpu.SemaphoreType.DMA
    vmem = pl.BlockSpec(memory_space=pltpu.VMEM)
    norm = float(tok * n_node * n_local) ** (-0.5)
    piece = pltpu.VMEM((n_local, head, share), F32)
    return pl.pallas_call(
        functools.partial(exchange_kernel, n_local, norm),
        out_shape=(
            jax.ShapeDtypeStruct((tok, head), BF16),
            jax.ShapeDtypeStruct((share, head), F32),
        ),
        in_specs=[pl.BlockSpec(memory_space=pltpu.HBM)] * 4,
        out_specs=(vmem, vmem),
        scratch_shapes=[
            pltpu.VMEM((tok, width), BF16),
            pltpu.VMEM((2, 2, 2, n_local, tok, share), BF16),
            pltpu.VMEM(codes.shape, BF16),
            pltpu.VMEM(scales.shape, F32),
            pltpu.VMEM(cotangent.shape, BF16),
            pltpu.VMEM((rows, head), BF16),
            pltpu.VMEM((n_local - 1, rows, head), BF16),
            pltpu.VMEM((n_local, 2, 4 * tok, share), BF16),
            pltpu.VMEM((head, tok), BF16),
            pltpu.VMEM((6, head, tok), BF16),
            piece, piece, piece, piece,
            pltpu.VMEM((tok, head), F32),
            dma((4,)), dma((n_local,)), dma((n_local,)), dma((5,)), dma((5,)),
            dma((n_local,)), dma((n_local,)), dma((n_local,)), dma((n_local,)),
            dma((n_local,)), dma((n_local,)),
            dma((n_local,)), dma((n_local,)),
        ],
        compiler_params=pltpu.CompilerParams(collective_id=0, has_side_effects=True),
        cost_estimate=pl.CostEstimate(
            flops=4 * tok * width * head, bytes_accessed=2 * tok * width, transcendentals=0
        ),
    )(activations, codes, scales, cotangent)


def gathered(n_node, n_local, activations, codes, scales, cotangent):
    head = codes.shape[2]
    stored = (codes.astype(F32) * scales[:, None, :]).astype(BF16).reshape(-1, head)
    weight = lax.all_gather(stored, "local", axis=0, tiled=True)
    values = jnp.dot(activations, weight, preferred_element_type=F32).astype(BF16)
    term = lax.dot_general(
        activations, cotangent, (((0,), (0,)), ((), ())), preferred_element_type=F32
    )
    tokens = activations.shape[0] * n_node * n_local
    term = term * float(tokens) ** (-0.5)
    share = term.shape[0] // (n_node * n_local)
    term = term.reshape(n_node, n_local, share, head)
    term = lax.psum_scatter(term, "local", scatter_dimension=1, tiled=True)
    term = lax.psum_scatter(term, "node", scatter_dimension=0, tiled=True)
    return values, term.reshape(share, head)


def solution(mesh):
    n_node, n_local = mesh.shape["node"], mesh.shape["local"]

    def on_device(activations, codes, scales, cotangent):
        share = activations.shape[1] // (n_node * n_local)
        rows = codes.shape[0] * codes.shape[1]
        tok = activations.shape[0]
        fits = n_node == 8 and n_local > 2 and share % 128 == 0 and rows % 256 == 0 and tok % 128 == 0
        run = exchanged if fits else gathered
        return run(n_node, n_local, activations, codes, scales, cotangent)

    return jax.shard_map(
        on_device,
        mesh=mesh,
        in_specs=(
            P(("node", "local"), None),
            P("local", None, None),
            P("local", None),
            P(("node", "local"), None),
        ),
        out_specs=(P(("node", "local"), None), P(("node", "local"), None)),
        check_vma=False,
    )
```

```python
import functools

import jax
import jax.numpy as jnp
from jax import lax
from jax.experimental import pallas as pl
from jax.experimental.pallas import tpu as pltpu
from jax.sharding import PartitionSpec as P

MESH = pl.DeviceIdType.MESH
F32 = jnp.float32
BF16 = jnp.bfloat16


def aligned(value, unit):
    return pl.multiple_of(value * unit, unit)


def exchange_kernel(
    n_local, norm,
    act_hbm, codes_hbm, scales_hbm, cot_hbm,
    values_ref, grad_ref,
    act, act_parts, codes_ref, scales_ref, cot_ref, weight, weight_in, act_in, cot_t, cot_in,
    other_out, other_in, term_out, term_in, total,
    load_sem, act_send, act_recv, cot_send, cot_recv,
    w_send, w_recv, f_send, f_recv, s_send, s_recv, g_send, g_recv,
):
    node, z = lax.axis_index("node"), lax.axis_index("local")
    y, x, core = node // 4, (node // 2) % 2, node % 2
    tok = act.shape[0]
    share = grad_ref.shape[0]
    blocks, block, _ = codes_ref.shape
    rows = blocks * block
    half = rows // 2
    last = n_local - 1

    loads = [
        pltpu.make_async_copy(there, here, load_sem.at[i])
        for i, (there, here) in enumerate((
            (codes_hbm, codes_ref), (scales_hbm, scales_ref),
            (cot_hbm, cot_ref), (act_hbm, act)))
    ]
    for load in loads:
        load.start()

    def at(to_y, to_x, to_core):
        return (to_y * 2 + to_x) * 2 + to_core

    partner = at(y, x, 1 - core)
    along_x = (at(y, 1 - x, core), at(y, 1 - x, 1 - core))
    along_y = (at(1 - y, x, core), at(1 - y, x, 1 - core))
    near = (partner,) + along_x + along_y
    line = [(k, (z + 1 + k) % n_local, (z + last - k) % n_local) for k in range(last)]

    barrier = pltpu.get_barrier_semaphore()
    for to in near:
        pl.semaphore_signal(barrier, inc=1, device_id=(to, z), device_id_type=MESH)
    for _, to, _ in line:
        pl.semaphore_signal(barrier, inc=1, device_id=(node, to), device_id_type=MESH)

    pl.semaphore_wait(barrier, len(near) + len(line))

    def send(src, dst, send_sem, recv_sem, to_node, to_local):
        return pltpu.make_async_remote_copy(
            src_ref=src, dst_ref=dst, send_sem=send_sem, recv_sem=recv_sem,
            device_id=(to_node, to_local), device_id_type=MESH)

    def cot_copy(i, source, slot, to):
        return send(source, cot_in.at[slot],
                    cot_send.at[i], cot_recv.at[i], to, z)

    cot_copies = [
        cot_copy(i, cot_t, slot, to)
        for i, (to, slot) in enumerate(((along_x[0], 0), (along_y[0], 4), (partner, 3)))
    ]
    cot_passes = [
        cot_copy(3 + i, cot_in.at[slot], slot + 1, partner)
        for i, slot in enumerate((0, 4))
    ]

    def second_of(k):
        return at(1 - y, x, core) if k % 2 == 0 else at(y, 1 - x, core)

    def column_of(k, owner):
        return pl.ds(aligned(owner * n_local + (z + 1 + k) % n_local, share), share)

    def chunks_of(k, to_y, to_x, to_core):
        owner = (z + 1 + k) % n_local
        if k % 2 == 0:
            return act_parts.at[:, to_x, to_core, owner]
        return act_parts.at[to_y, :, to_core, owner]

    def act_copies(k):
        over_x = k % 2 == 0
        first = (y, 1 - x) if over_x else (1 - y, x)
        own_row, first_row = (2, 0) if over_x else (0, 2)
        copies = []
        for to_y, to_x, to_core, row in (
            (first[0], first[1], core, first_row),
            (first[0], first[1], 1 - core, first_row + 1),
            (y, x, 1 - core, own_row + 1),
        ):
            place = pl.ds(row * tok, tok)
            if k < 2:
                pairs = [
                    (act_hbm.at[:, column_of(k, at(i, to_x, to_core) if over_x else at(to_y, i, to_core))],
                     act_in.at[k, i, place])
                    for i in range(2)
                ]
            else:
                pairs = [(chunks_of(k, to_y, to_x, to_core), act_in.at[k, :, place])]
            for src, dst in pairs:
                copies.append(send(src, dst, act_send.at[k], act_recv.at[k],
                                   at(to_y, to_x, to_core), z))
        return copies

    def act_whole(k):
        ref = act_in.at[k, :, 0 : 3 * tok]
        return send(ref, ref, act_send.at[k], act_recv.at[k], partner, z)

    def sum_copy(k):
        return send(other_out.at[k], other_in.at[k], s_send.at[k], s_recv.at[k],
                    second_of(k), z)

    def term_copy(k, to):
        return send(term_out.at[k], term_in.at[k], g_send.at[k], g_recv.at[k], node, to)

    def half_of(of_core):
        return pl.ds(aligned(of_core, half), half)

    def line_copy(k, to):
        part = half_of(core)
        return send(weight.at[part], weight_in.at[k, part], w_send.at[k], w_recv.at[k], node, to)

    def pass_copy(k, of_core):
        ref = weight_in.at[k, half_of(of_core)]
        return send(ref, ref, f_send.at[k], f_recv.at[k], partner, z)

    for copy in act_copies(0) + act_copies(1):
        copy.start()
    loads[2].wait()
    cot_t[...] = cot_ref[...].T
    for copy in cot_copies:
        copy.start()
    loads[0].wait()
    loads[1].wait()
    for b in range(blocks):
        part = codes_ref[b].astype(F32) * scales_ref[b : b + 1, :]
        weight[b * block : (b + 1) * block, :] = part.astype(BF16)
    for k, to, _ in line:
        line_copy(k, to).start()
    loads[3].wait()
    for i in range(8):
        for j in range(n_local):
            column = (i * n_local + j) * share
            act_parts[i // 4, (i // 2) % 2, i % 2, j] = act[:, column : column + share]
    cot_in[2] = cot_t[...]

    def projected(owner, stored):
        return jnp.dot(act[:, pl.ds(aligned(owner, rows), rows)], stored, preferred_element_type=F32)

    total[...] = projected(z, weight[...])

    def group_term(k):
        over_x = k % 2 == 0
        own_row = 2 if over_x else 0
        own = slice(own_row * tok, (own_row + 1) * tok)
        act_in[k, :, own, :] = chunks_of(k, y, x, core)[...]
        if k == 0:
            for i, copy in enumerate(cot_copies):
                copy.wait_recv()
                if i < 2:
                    cot_passes[i].start()
            if n_local > 2:
                for copy in act_copies(2):
                    copy.start()
        act_whole(k).wait_recv()
        if k == 0:
            for copy in cot_passes:
                copy.wait_recv()
        begin = 0 if over_x else 2
        mine = y if over_x else x
        cot = jnp.concatenate([cot_in[begin + i] for i in range(4)], axis=1)
        other_out[k] = jnp.dot(cot, act_in[k, 1 - mine], preferred_element_type=F32)
        sum_copy(k).start()
        if k + 3 < n_local:
            for copy in act_copies(k + 3):
                copy.start()
        term_out[k] = jnp.dot(cot, act_in[k, mine], preferred_element_type=F32)

    def finish_term(k):
        sum_copy(k).wait_recv()
        term_out[k] += other_in[k]
        if k < last:
            term_copy(k, line[k][1]).start()

    def add_half(k, owner, of_core):
        column = aligned(owner * 2 + of_core, half)
        total[...] += jnp.dot(act[:, pl.ds(column, half)], weight_in[k, half_of(of_core)],
                              preferred_element_type=F32)

    group_term(0)
    for k in range(1, last):
        group_term(k)
        finish_term(k - 1)
    finish_term(last - 1)
    group_term(last)
    for k, to, owner in line:
        line_copy(k, to).wait_recv()
        pass_copy(k, core).start()
        add_half(k, owner, core)
    for copy in cot_copies + cot_passes:
        copy.wait_send()
    for k in range(n_local):
        act_whole(k).wait_send()
    for k, to, owner in line:
        line_copy(k, to).wait_send()
        pass_copy(k, 1 - core).wait_recv()
        add_half(k, owner, 1 - core)
    values_ref[...] = total[...].astype(BF16)
    finish_term(last)
    for k, _, _ in line:
        pass_copy(k, core).wait_send()
    for k in range(n_local):
        sum_copy(k).wait_send()
    grad = term_out[last]
    for k, to, _ in line:
        term_copy(k, to).wait_recv()
        grad += term_in[k]
    grad_ref[...] = grad.T * norm
    for k, to, _ in line:
        term_copy(k, to).wait_send()


def exchanged(n_node, n_local, activations, codes, scales, cotangent):
    tok, width = activations.shape
    blocks, block, head = codes.shape
    rows = blocks * block
    share = width // (n_node * n_local)
    dma = pltpu.SemaphoreType.DMA
    vmem = pl.BlockSpec(memory_space=pltpu.VMEM)
    norm = float(tok * n_node * n_local) ** (-0.5)
    piece = pltpu.VMEM((n_local, head, share), F32)
    return pl.pallas_call(
        functools.partial(exchange_kernel, n_local, norm),
        out_shape=(
            jax.ShapeDtypeStruct((tok, head), BF16),
            jax.ShapeDtypeStruct((share, head), F32),
        ),
        in_specs=[pl.BlockSpec(memory_space=pltpu.HBM)] * 4,
        out_specs=(vmem, vmem),
        scratch_shapes=[
            pltpu.VMEM((tok, width), BF16),
            pltpu.VMEM((2, 2, 2, n_local, tok, share), BF16),
            pltpu.VMEM(codes.shape, BF16),
            pltpu.VMEM(scales.shape, F32),
            pltpu.VMEM(cotangent.shape, BF16),
            pltpu.VMEM((rows, head), BF16),
            pltpu.VMEM((n_local - 1, rows, head), BF16),
            pltpu.VMEM((n_local, 2, 4 * tok, share), BF16),
            pltpu.VMEM((head, tok), BF16),
            pltpu.VMEM((6, head, tok), BF16),
            piece, piece, piece, piece,
            pltpu.VMEM((tok, head), F32),
            dma((4,)), dma((n_local,)), dma((n_local,)), dma((5,)), dma((5,)),
            dma((n_local,)), dma((n_local,)), dma((n_local,)), dma((n_local,)),
            dma((n_local,)), dma((n_local,)),
            dma((n_local,)), dma((n_local,)),
        ],
        compiler_params=pltpu.CompilerParams(collective_id=0, has_side_effects=True),
        cost_estimate=pl.CostEstimate(
            flops=4 * tok * width * head, bytes_accessed=2 * tok * width, transcendentals=0
        ),
    )(activations, codes, scales, cotangent)


def gathered(n_node, n_local, activations, codes, scales, cotangent):
    head = codes.shape[2]
    stored = (codes.astype(F32) * scales[:, None, :]).astype(BF16).reshape(-1, head)
    weight = lax.all_gather(stored, "local", axis=0, tiled=True)
    values = jnp.dot(activations, weight, preferred_element_type=F32).astype(BF16)
    term = lax.dot_general(
        activations, cotangent, (((0,), (0,)), ((), ())), preferred_element_type=F32
    )
    tokens = activations.shape[0] * n_node * n_local
    term = term * float(tokens) ** (-0.5)
    share = term.shape[0] // (n_node * n_local)
    term = term.reshape(n_node, n_local, share, head)
    term = lax.psum_scatter(term, "local", scatter_dimension=1, tiled=True)
    term = lax.psum_scatter(term, "node", scatter_dimension=0, tiled=True)
    return values, term.reshape(share, head)


def solution(mesh):
    n_node, n_local = mesh.shape["node"], mesh.shape["local"]

    def on_device(activations, codes, scales, cotangent):
        share = activations.shape[1] // (n_node * n_local)
        rows = codes.shape[0] * codes.shape[1]
        tok = activations.shape[0]
        fits = n_node == 8 and n_local > 1 and share % 128 == 0 and rows % 256 == 0 and tok % 128 == 0
        run = exchanged if fits else gathered
        return run(n_node, n_local, activations, codes, scales, cotangent)

    return jax.shard_map(
        on_device,
        mesh=mesh,
        in_specs=(
            P(("node", "local"), None),
            P("local", None, None),
            P("local", None),
            P(("node", "local"), None),
        ),
        out_specs=(P(("node", "local"), None), P(("node", "local"), None)),
        check_vma=False,
    )
```

```python
import functools

import jax
import jax.numpy as jnp
from jax import lax
from jax.experimental import pallas as pl
from jax.experimental.pallas import tpu as pltpu
from jax.sharding import PartitionSpec as P

MESH = pl.DeviceIdType.MESH
F32 = jnp.float32
BF16 = jnp.bfloat16


def aligned(value, unit):
    return pl.multiple_of(value * unit, unit)


def exchange_kernel(
    n_local, norm,
    act_hbm, codes_hbm, scales_hbm, cot_hbm,
    values_ref, grad_ref,
    act, act_parts, codes_ref, scales_ref, cot_ref, weight, weight_in, act_in, cot_t, cot_in,
    other_out, other_in, term_out, term_in, total,
    load_sem, act_send, act_recv, cot_send, cot_recv,
    w_send, w_recv, f_send, f_recv, s_send, s_recv, g_send, g_recv,
):
    node, z = lax.axis_index("node"), lax.axis_index("local")
    y, x, core = node // 4, (node // 2) % 2, node % 2
    tok = act.shape[0]
    share = grad_ref.shape[0]
    blocks, block, _ = codes_ref.shape
    rows = blocks * block
    half = rows // 2
    last = n_local - 1

    loads = [
        pltpu.make_async_copy(there, here, load_sem.at[i])
        for i, (there, here) in enumerate((
            (codes_hbm, codes_ref), (scales_hbm, scales_ref),
            (cot_hbm, cot_ref), (act_hbm, act)))
    ]
    for load in loads:
        load.start()

    def at(to_y, to_x, to_core):
        return (to_y * 2 + to_x) * 2 + to_core

    partner = at(y, x, 1 - core)
    along_x = (at(y, 1 - x, core), at(y, 1 - x, 1 - core))
    along_y = (at(1 - y, x, core), at(1 - y, x, 1 - core))
    near = (partner,) + along_x + along_y
    line = [(k, (z + 1 + k) % n_local, (z + last - k) % n_local) for k in range(last)]

    barrier = pltpu.get_barrier_semaphore()
    for to in near:
        pl.semaphore_signal(barrier, inc=1, device_id=(to, z), device_id_type=MESH)
    for _, to, _ in line:
        pl.semaphore_signal(barrier, inc=1, device_id=(node, to), device_id_type=MESH)

    pl.semaphore_wait(barrier, len(near) + len(line))

    def send(src, dst, send_sem, recv_sem, to_node, to_local):
        return pltpu.make_async_remote_copy(
            src_ref=src, dst_ref=dst, send_sem=send_sem, recv_sem=recv_sem,
            device_id=(to_node, to_local), device_id_type=MESH)

    def cot_copy(i, source, slot, to):
        return send(source, cot_in.at[slot],
                    cot_send.at[i], cot_recv.at[i], to, z)

    cot_copies = [
        cot_copy(i, cot_t, slot, to)
        for i, (to, slot) in enumerate(((along_x[0], 0), (along_y[0], 4), (partner, 3)))
    ]
    cot_passes = [
        cot_copy(3 + i, cot_in.at[slot], slot + 1, partner)
        for i, slot in enumerate((0, 4))
    ]

    def second_of(k):
        return at(1 - y, x, core) if k % 2 == 0 else at(y, 1 - x, core)

    def column_of(k, owner):
        return pl.ds(aligned(owner * n_local + (z + 1 + k) % n_local, share), share)

    def chunks_of(k, to_y, to_x, to_core):
        owner = (z + 1 + k) % n_local
        if k % 2 == 0:
            return act_parts.at[:, to_x, to_core, owner]
        return act_parts.at[to_y, :, to_core, owner]

    def act_copies(k):
        over_x = k % 2 == 0
        first = (y, 1 - x) if over_x else (1 - y, x)
        own_row, first_row = (2, 0) if over_x else (0, 2)
        copies = []
        for to_y, to_x, to_core, row in (
            (first[0], first[1], core, first_row),
            (first[0], first[1], 1 - core, first_row + 1),
            (y, x, 1 - core, own_row + 1),
        ):
            place = pl.ds(row * tok, tok)
            if k < 2:
                pairs = [
                    (act_hbm.at[:, column_of(k, at(i, to_x, to_core) if over_x else at(to_y, i, to_core))],
                     act_in.at[k, i, place])
                    for i in range(2)
                ]
            else:
                pairs = [(chunks_of(k, to_y, to_x, to_core), act_in.at[k, :, place])]
            for src, dst in pairs:
                copies.append(send(src, dst, act_send.at[k], act_recv.at[k],
                                   at(to_y, to_x, to_core), z))
        return copies

    def act_whole(k):
        ref = act_in.at[k, :, 0 : 3 * tok]
        return send(ref, ref, act_send.at[k], act_recv.at[k], partner, z)

    def sum_copy(k):
        return send(other_out.at[k], other_in.at[k], s_send.at[k], s_recv.at[k],
                    second_of(k), z)

    def term_copy(k, to):
        return send(term_out.at[k], term_in.at[k], g_send.at[k], g_recv.at[k], node, to)

    def half_of(of_core):
        return pl.ds(aligned(of_core, half), half)

    def line_copy(k, to):
        part = half_of(core)
        return send(weight.at[part], weight_in.at[k, part], w_send.at[k], w_recv.at[k], node, to)

    def pass_copy(k, of_core):
        ref = weight_in.at[k, half_of(of_core)]
        return send(ref, ref, f_send.at[k], f_recv.at[k], partner, z)

    for copy in act_copies(0) + act_copies(1):
        copy.start()
    loads[2].wait()
    cot_t[...] = cot_ref[...].T
    for copy in cot_copies:
        copy.start()
    loads[0].wait()
    loads[1].wait()
    for b in range(blocks):
        part = codes_ref[b].astype(F32) * scales_ref[b : b + 1, :]
        weight[b * block : (b + 1) * block, :] = part.astype(BF16)
    for k, to, _ in line:
        line_copy(k, to).start()
    loads[3].wait()
    for i in range(8):
        for j in range(n_local):
            column = (i * n_local + j) * share
            act_parts[i // 4, (i // 2) % 2, i % 2, j] = act[:, column : column + share]
    cot_in[2] = cot_t[...]

    def projected(owner, stored):
        return jnp.dot(act[:, pl.ds(aligned(owner, rows), rows)], stored, preferred_element_type=F32)

    total[...] = projected(z, weight[...])

    def group_term(k):
        over_x = k % 2 == 0
        own_row = 2 if over_x else 0
        own = slice(own_row * tok, (own_row + 1) * tok)
        act_in[k, :, own, :] = chunks_of(k, y, x, core)[...]
        if k == 0:
            for i, copy in enumerate(cot_copies):
                copy.wait_recv()
                if i < 2:
                    cot_passes[i].start()
        act_whole(k).wait_recv()
        if k == 0:
            for copy in cot_passes:
                copy.wait_recv()
        begin = 0 if over_x else 2
        mine = y if over_x else x
        cot = jnp.concatenate([cot_in[begin + i] for i in range(4)], axis=1)
        other_out[k] = jnp.dot(cot, act_in[k, 1 - mine], preferred_element_type=F32)
        sum_copy(k).start()
        if k + 2 < n_local:
            for copy in act_copies(k + 2):
                copy.start()
        term_out[k] = jnp.dot(cot, act_in[k, mine], preferred_element_type=F32)

    def finish_term(k):
        sum_copy(k).wait_recv()
        term_out[k] += other_in[k]
        if k < last:
            term_copy(k, line[k][1]).start()

    def add_half(k, owner, of_core):
        column = aligned(owner * 2 + of_core, half)
        total[...] += jnp.dot(act[:, pl.ds(column, half)], weight_in[k, half_of(of_core)],
                              preferred_element_type=F32)

    group_term(0)
    for k in range(1, last):
        group_term(k)
        finish_term(k - 1)
    finish_term(last - 1)
    group_term(last)
    for k, to, owner in line:
        line_copy(k, to).wait_recv()
        pass_copy(k, core).start()
        add_half(k, owner, core)
    for copy in cot_copies + cot_passes:
        copy.wait_send()
    for k in range(n_local):
        act_whole(k).wait_send()
    for k, to, owner in line:
        line_copy(k, to).wait_send()
        pass_copy(k, 1 - core).wait_recv()
        add_half(k, owner, 1 - core)
    values_ref[...] = total[...].astype(BF16)
    finish_term(last)
    for k, _, _ in line:
        pass_copy(k, core).wait_send()
    for k in range(n_local):
        sum_copy(k).wait_send()
    grad = term_out[last]
    for k, to, _ in line:
        term_copy(k, to).wait_recv()
        grad += term_in[k]
    grad_ref[...] = grad.T * norm
    for k, to, _ in line:
        term_copy(k, to).wait_send()


def exchanged(n_node, n_local, activations, codes, scales, cotangent):
    tok, width = activations.shape
    blocks, block, head = codes.shape
    rows = blocks * block
    share = width // (n_node * n_local)
    dma = pltpu.SemaphoreType.DMA
    vmem = pl.BlockSpec(memory_space=pltpu.VMEM)
    norm = float(tok * n_node * n_local) ** (-0.5)
    piece = pltpu.VMEM((n_local, head, share), F32)
    return pl.pallas_call(
        functools.partial(exchange_kernel, n_local, norm),
        out_shape=(
            jax.ShapeDtypeStruct((tok, head), BF16),
            jax.ShapeDtypeStruct((share, head), F32),
        ),
        in_specs=[pl.BlockSpec(memory_space=pltpu.HBM)] * 4,
        out_specs=(vmem, vmem),
        scratch_shapes=[
            pltpu.VMEM((tok, width), BF16),
            pltpu.VMEM((2, 2, 2, n_local, tok, share), BF16),
            pltpu.VMEM(codes.shape, BF16),
            pltpu.VMEM(scales.shape, F32),
            pltpu.VMEM(cotangent.shape, BF16),
            pltpu.VMEM((rows, head), BF16),
            pltpu.VMEM((n_local - 1, rows, head), BF16),
            pltpu.VMEM((n_local, 2, 4 * tok, share), BF16),
            pltpu.VMEM((head, tok), BF16),
            pltpu.VMEM((6, head, tok), BF16),
            piece, piece, piece, piece,
            pltpu.VMEM((tok, head), F32),
            dma((4,)), dma((n_local,)), dma((n_local,)), dma((5,)), dma((5,)),
            dma((n_local,)), dma((n_local,)), dma((n_local,)), dma((n_local,)),
            dma((n_local,)), dma((n_local,)),
            dma((n_local,)), dma((n_local,)),
        ],
        compiler_params=pltpu.CompilerParams(collective_id=0, has_side_effects=True),
        cost_estimate=pl.CostEstimate(
            flops=4 * tok * width * head, bytes_accessed=2 * tok * width, transcendentals=0
        ),
    )(activations, codes, scales, cotangent)


def gathered(n_node, n_local, activations, codes, scales, cotangent):
    head = codes.shape[2]
    stored = (codes.astype(F32) * scales[:, None, :]).astype(BF16).reshape(-1, head)
    weight = lax.all_gather(stored, "local", axis=0, tiled=True)
    values = jnp.dot(activations, weight, preferred_element_type=F32).astype(BF16)
    term = lax.dot_general(
        activations, cotangent, (((0,), (0,)), ((), ())), preferred_element_type=F32
    )
    tokens = activations.shape[0] * n_node * n_local
    term = term * float(tokens) ** (-0.5)
    share = term.shape[0] // (n_node * n_local)
    term = term.reshape(n_node, n_local, share, head)
    term = lax.psum_scatter(term, "local", scatter_dimension=1, tiled=True)
    term = lax.psum_scatter(term, "node", scatter_dimension=0, tiled=True)
    return values, term.reshape(share, head)


def solution(mesh):
    n_node, n_local = mesh.shape["node"], mesh.shape["local"]

    def on_device(activations, codes, scales, cotangent):
        share = activations.shape[1] // (n_node * n_local)
        rows = codes.shape[0] * codes.shape[1]
        tok = activations.shape[0]
        fits = n_node == 8 and n_local > 1 and share % 128 == 0 and rows % 256 == 0 and tok % 128 == 0
        run = exchanged if fits else gathered
        return run(n_node, n_local, activations, codes, scales, cotangent)

    return jax.shard_map(
        on_device,
        mesh=mesh,
        in_specs=(
            P(("node", "local"), None),
            P("local", None, None),
            P("local", None),
            P(("node", "local"), None),
        ),
        out_specs=(P(("node", "local"), None), P(("node", "local"), None)),
        check_vma=False,
    )
```
